32 devices in a mesh: freq: 4 (over z), row: 2 (over x), col: 4 (over y, core).
Axes of the slice: x: 2, y: 2, z: 4, core: 2. Of those that a mesh axis runs over, the one named last changes fastest.
Arguments:
- samples: int32 [2, 2048, 68608], P(None, ('row', 'col', 'freq')), may hold values from -7 to 7
- input_gains: float32 [2048], P(('row', 'col', 'freq')), may hold values from 0.3 to 3
- filter_taps: float32 [4, 1024], replicated, may hold values from 0.25 to 1
Outputs:
- vis_real: bfloat16 [16, 2048, 2048], P('freq', 'row', 'col')
- vis_imag: bfloat16 [16, 2048, 2048], P('freq', 'row', 'col')
The draws below stay inside these ranges and needn't reach their ends.
All inputs are finite; a program needn't handle non-finite values.
Results may differ from the reference program's by a relative error of at most 0.0065.
Values may be sent and summed in bfloat16 or wider, within the bound.
No kernel may reach another device: no remote copies, remote signals or barrier semaphores. Data moves between devices by JAX's collectives and lax.ppermute only.
A program may use at most 192 MiB of HBM per device.

```python
import math
import jax
import jax.numpy as jnp
from jax import lax

INPUTS = 2048
NFFT = 1024
TAPS = 4
SPEC = 64
BAND = 16
NSAMP = 68608


def plant(entries, own_key, smallest, largest):
    spot = [jax.random.randint(jax.random.fold_in(own_key, axis), (), 0, length) for axis, length in enumerate(entries.shape)]
    main_axis = entries.shape.index(max(entries.shape))
    neighbour = spot[:main_axis] + [(spot[main_axis] + 1) % entries.shape[main_axis]] + spot[main_axis + 1:]
    return entries.at[tuple(spot)].set(smallest).at[tuple(neighbour)].set(largest)


def levels(stream_key, dims, pieces, low, high):
    loudness, own = 1.0, jax.random.fold_in(stream_key, 6)
    for dim, shards_of in pieces:
        heights = jnp.exp(jax.random.uniform(jax.random.fold_in(own, dim), (shards_of,), jnp.float32, low / len(pieces), high / len(pieces)))
        loudness = loudness * jnp.repeat(heights, dims[dim] // shards_of).reshape([-1 if axis == dim else 1 for axis in range(len(dims))])
    return loudness


def setup_inputs(seed: int = 0) -> dict:
    seeds = jax.random.split(jax.random.key(seed), 4)
    return {
        "samples": plant(jax.random.randint(seeds[0], (2, INPUTS, NSAMP), -7, 8), jax.random.fold_in(seeds[0], 1), -7, 7).astype(jnp.int32),
        "input_gains": jnp.clip(jnp.exp(math.log(3.0) - 2.3025851 * jax.random.uniform(seeds[1], (INPUTS,), jnp.float32) ** levels(seeds[1], (INPUTS,), ((0, 32),), -0.2, 0.2)), 0.3, 3.0),
        "filter_taps": jnp.clip(jax.random.uniform(seeds[2], (TAPS, NFFT), jnp.float32, 0.25, 1.0), 0.25, 1.0),
    }


def dft_table(channels):
    position = jnp.arange(NFFT, dtype=jnp.int32)
    channel = jnp.arange(channels, dtype=jnp.int32)
    phases = (position[:, None] * channel[None, :] % NFFT).astype(jnp.float32) * (2.0 * math.pi / NFFT)
    scaling = 0.5 / math.sqrt(NFFT)
    cosine = jnp.cos(phases) * scaling
    sine = jnp.sin(phases) * scaling
    real_rows = jnp.stack([cosine, -sine], axis=1)
    imag_rows = jnp.stack([sine, cosine], axis=1)
    return jnp.stack([real_rows, imag_rows], axis=0).astype(jnp.bfloat16)

def reference(samples, input_gains, filter_taps):
    table_values = dft_table(BAND).astype(jnp.float32)
    count = INPUTS // 64

    def one_block(block_index):
        start = (block_index * 64).astype(jnp.int32)
        segment = lax.dynamic_slice_in_dim(samples, start, 64, 1)
        block_gains = lax.dynamic_slice_in_dim(input_gains, start, 64, 0)
        voltage = segment.astype(jnp.float32) * 0.25 * block_gains[None, :, None]
        frames = voltage.reshape(2, 64, SPEC + TAPS - 1, NFFT)
        filtered = frames[:, :, 0:SPEC, :] * filter_taps[0]
        for tap_index in range(1, TAPS):
            filtered = filtered + frames[:, :, tap_index:tap_index + SPEC, :] * filter_taps[tap_index]
        filtered = filtered.astype(jnp.bfloat16)
        spectra = jnp.einsum('pimn,pnqk->kiqm', filtered.astype(jnp.float32), table_values)
        return spectra.reshape(BAND, 64, 2 * SPEC).astype(jnp.bfloat16)
    blocks = lax.map(one_block, jnp.arange(count, dtype=jnp.int32))
    spectra = jnp.transpose(blocks, (1, 0, 2, 3)).reshape(BAND, INPUTS, 2 * SPEC)

    def one_channel(channel_data):
        rotated = jnp.concatenate([-channel_data[:, SPEC:], channel_data[:, :SPEC]], axis=1)
        real_part = jnp.dot(channel_data, channel_data.T, preferred_element_type=jnp.float32) * (1.0 / SPEC)
        imag_part = jnp.dot(channel_data, rotated.T, preferred_element_type=jnp.float32) * (1.0 / SPEC)
        return (real_part.astype(jnp.bfloat16), imag_part.astype(jnp.bfloat16))
    vis_real, vis_imag = lax.map(one_channel, spectra)
    return (vis_real, vis_imag)
```

```python
import functools
import math

import jax
import jax.numpy as jnp
import numpy as np
from jax import lax
from jax.experimental import pallas as pl
from jax.experimental.pallas import tpu as pltpu
from jax.sharding import PartitionSpec as P

NFFT = 1024
TAPS = 4
SPEC = 64
CH_DEV = 4
LANES = 128
VMEM_BYTES = 60 * 2**20


def dft_rows(channels):
    phases = (np.arange(channels)[:, None] * np.arange(NFFT)[None, :] % NFFT) * (
        2.0 * math.pi / NFFT
    )
    scaling = 0.5 / math.sqrt(NFFT)
    cosine = np.cos(phases) * scaling
    sine = np.sin(phases) * scaling
    real_rows = np.concatenate([cosine, sine], axis=1)
    imag_rows = np.concatenate([-sine, cosine], axis=1)
    rows = np.stack([real_rows, imag_rows], axis=1).reshape(2 * channels, 2 * NFFT)
    return jnp.asarray(rows.astype(np.float32)).astype(jnp.bfloat16)


def channelize_body(
    gain_ref, taps_ref, table_ref, samples_ref, *rest, first, half, blocks, groups
):
    outs, (weights, raw, lhs, sums, held, sems) = rest[:groups], rest[groups:]
    inputs = samples_ref.shape[1]
    rows = table_ref.shape[0]
    pieces = []
    for index, (start, stop) in enumerate(blocks):
        pieces.append((index, 0, start, min(stop, half)))
        pieces.append((index, 1, half + start, half + stop))
    copies = {}
    for index, side, begin, end in pieces:
        if begin < end:
            span = pl.ds(begin * NFFT, (end - begin) * NFFT)
            source = pl.ds((first + begin) * NFFT, (end - begin) * NFFT)
            copies[index, side] = pltpu.make_async_copy(
                samples_ref.at[:, :, source], raw.at[:, :, span], sems.at[index, side]
            )
            copies[index, side].start()
    for p in range(2):
        for b in range(NFFT // LANES):
            table = table_ref[:, p * NFFT + b * LANES : p * NFFT + (b + 1) * LANES].astype(
                jnp.float32
            )
            for t in range(TAPS):
                exact = table * taps_ref[t : t + 1, b * LANES : (b + 1) * LANES]
                high = exact.astype(jnp.bfloat16)
                low = (exact - high.astype(jnp.float32)).astype(jnp.bfloat16)
                at = pl.ds(p * NFFT + b * LANES, LANES)
                weights[t * rows : (t + 1) * rows, at] = high
                weights[(TAPS + t) * rows : (TAPS + t + 1) * rows, at] = low
    for index, (start, stop) in enumerate(blocks):
        for side in range(2):
            if (index, side) in copies:
                copies[index, side].wait()
        buffer = lhs[index % 2]
        for slot in range(start, stop):
            for side in range(2):
                frame = side * half + slot
                to = (slot - start) * 2 * inputs + side * inputs
                for p in range(2):
                    buffer[to : to + inputs, p * NFFT : (p + 1) * NFFT] = (
                        raw[p, :, frame * NFFT : (frame + 1) * NFFT]
                        .astype(jnp.float32)
                        .astype(jnp.bfloat16)
                    )
        size = (stop - start) * 2 * inputs
        both = lax.dot_general(
            weights[...],
            buffer[0:size, :],
            (((1,), (1,)), ((), ())),
            preferred_element_type=jnp.float32,
        )
        sums[:, start * LANES : stop * LANES] = both[: TAPS * rows] + both[TAPS * rows :]
    gain = gain_ref[...]
    gain = jnp.concatenate([gain, gain], axis=1) * (0.25 / math.sqrt(SPEC))
    for slot in range(half):
        total = sums[0:rows, slot * LANES : (slot + 1) * LANES]
        for t in range(1, TAPS):
            total = total + sums[
                t * rows : (t + 1) * rows, (slot + t) * LANES : (slot + t + 1) * LANES
            ]
        held[pl.ds(slot, rows, stride=half), :] = total * gain
    me = lax.axis_index("freq")
    depth = 2 * half
    for s in range(groups):
        to = lax.rem(me + s, groups) * (CH_DEV * depth)
        for k in range(CH_DEV):
            outs[s][k] = held[
                pl.ds(pl.multiple_of(to + k * depth, 8), depth), :
            ].astype(jnp.bfloat16)


def channelize(samples, gains, taps, first, half, cuts, groups):
    inputs = samples.shape[1]
    channels = CH_DEV * groups
    rows = 2 * channels
    slots = half + TAPS - 1
    blocks = list(zip(cuts[:-1], cuts[1:]))
    widest = max(stop - start for start, stop in blocks)
    frames = 2 * half + TAPS - 1
    return pl.pallas_call(
        functools.partial(
            channelize_body, first=first, half=half, blocks=blocks, groups=groups
        ),
        grid=(1,),
        in_specs=[
            pl.BlockSpec((1, inputs), lambda i: (0, 0)),
            pl.BlockSpec((TAPS, NFFT), lambda i: (0, 0)),
            pl.BlockSpec((rows, 2 * NFFT), lambda i: (0, 0)),
            pl.BlockSpec(memory_space=pl.ANY),
        ],
        out_specs=[pl.BlockSpec((CH_DEV, 2 * half, LANES), lambda i: (0, 0, 0))] * groups,
        out_shape=[jax.ShapeDtypeStruct((CH_DEV, 2 * half, LANES), jnp.bfloat16)] * groups,
        scratch_shapes=[
            pltpu.VMEM((2 * TAPS * rows, 2 * NFFT), jnp.bfloat16),
            pltpu.VMEM((2, inputs, frames * NFFT), jnp.int32),
            [pltpu.VMEM((widest * 2 * inputs, 2 * NFFT), jnp.bfloat16)] * 2,
            pltpu.VMEM((TAPS * rows, slots * LANES), jnp.float32),
            pltpu.VMEM((rows * half, LANES), jnp.float32),
            pltpu.SemaphoreType.DMA((len(blocks), 2)),
        ],
        compiler_params=pltpu.CompilerParams(vmem_limit_bytes=VMEM_BYTES),
        cost_estimate=pl.CostEstimate(
            flops=2 * 2 * NFFT * 256 * frames * inputs,
            bytes_accessed=8 * inputs * frames * NFFT,
            transcendentals=0,
        ),
        name="channelize",
    )(gains.reshape(1, inputs), taps, dft_rows(channels), samples)


def regroup_body(*refs, half):
    groups = len(refs) - 2
    sources, out, ordered = refs[:groups], refs[groups], refs[groups + 1]
    me = lax.axis_index("freq")
    for s in range(groups):
        ordered[lax.rem(me - s + groups, groups)] = sources[s][...]
    depth = 2 * half
    lane = lax.broadcasted_iota(jnp.int32, (depth, LANES), 1)
    for pair in range(groups // 2):
        for k in range(CH_DEV):
            left = ordered[2 * pair, k].astype(jnp.float32)
            right = ordered[2 * pair + 1, k].astype(jnp.float32)
            early = jnp.where(lane < LANES // 2, left, pltpu.roll(right, LANES // 2, 1))
            late = jnp.where(lane < LANES // 2, pltpu.roll(left, LANES // 2, 1), right)
            at = pl.ds(pair * LANES, LANES)
            out[k, 0:depth, at] = early.astype(jnp.bfloat16)
            out[k, depth : 2 * depth, at] = late.astype(jnp.bfloat16)


def regroup(sources, half):
    groups = len(sources)
    shape = (CH_DEV, 4 * half, groups * LANES // 2)
    return pl.pallas_call(
        functools.partial(regroup_body, half=half),
        out_shape=jax.ShapeDtypeStruct(shape, jnp.bfloat16),
        scratch_shapes=[pltpu.VMEM((groups,) + sources[0].shape, jnp.bfloat16)],
        name="regroup",
    )(*sources)


def products_body(*refs, half, parts):
    rows_in = [refs[4 * part : 4 * part + 4] for part in range(parts)]
    cols_in = [refs[4 * parts + 2 * part : 4 * parts + 2 * part + 2] for part in range(parts)]
    real, imag, left, right = refs[6 * parts :]
    row, col = lax.axis_index("row"), lax.axis_index("col")
    y, core = col // 2, lax.rem(col, 2)
    width = rows_in[0][0].shape[2]
    deep = 4 * half
    for part in range(parts):
        down = slice(part * deep, (part + 1) * deep)
        for flip_y in range(2):
            for flip_core in range(2):
                block = (y + flip_y) % 2 * 2 + (core + flip_core) % 2
                left[block, down, :] = rows_in[part][2 * flip_y + flip_core][0]
    for t in range(2):
        across = slice(t * width, (t + 1) * width)

        @pl.when(row == y)
        def _():
            right[:, across] = left[core * 2 + t]

        @pl.when(row != y)
        def _():
            for part in range(parts):
                down = slice(part * deep, (part + 1) * deep)
                right[down, across] = cols_in[part][t][0]

    columns = 2 * width
    for at in range(0, parts * deep, 2 * half):
        re, im = right[at : at + half, 0:columns], right[at + half : at + 2 * half, 0:columns]
        right[at : at + half, columns : 2 * columns] = -im
        right[at + half : at + 2 * half, columns : 2 * columns] = re
    for block in range(4):
        product = lax.dot_general(
            left[block],
            right[...],
            (((0,), (0,)), ((), ())),
            preferred_element_type=jnp.float32,
        )
        at = slice(block * width, (block + 1) * width)
        real[0, at, :] = product[:, 0:columns].astype(jnp.bfloat16)
        imag[0, at, :] = product[:, columns : 2 * columns].astype(jnp.bfloat16)


def products(row_blocks, col_blocks, half):
    parts = len(row_blocks)
    _, deep, width = row_blocks[0][0].shape
    flat = [a for part in row_blocks for a in part] + [a for part in col_blocks for a in part]
    out = jax.ShapeDtypeStruct((CH_DEV, 4 * width, 2 * width), jnp.bfloat16)
    return pl.pallas_call(
        functools.partial(products_body, half=half, parts=parts),
        grid=(CH_DEV,),
        in_specs=[pl.BlockSpec((1, deep, width), lambda k: (k, 0, 0))] * len(flat),
        out_specs=[pl.BlockSpec((1, 4 * width, 2 * width), lambda k: (k, 0, 0))] * 2,
        out_shape=[out, out],
        scratch_shapes=[
            pltpu.VMEM((4, parts * deep, width), jnp.bfloat16),
            pltpu.VMEM((parts * deep, 4 * width), jnp.bfloat16),
        ],
        compiler_params=pltpu.CompilerParams(vmem_limit_bytes=VMEM_BYTES),
        cost_estimate=pl.CostEstimate(
            flops=2 * CH_DEV * parts * deep * 16 * width * width,
            bytes_accessed=2 * 2 * CH_DEV * 8 * width * width,
            transcendentals=0,
        ),
        name="products",
    )(*flat)


def exchange(sent, groups):
    ring = lambda s: [(i, (i + s) % groups) for i in range(groups)]
    turned = [sent[0]] + [lax.ppermute(sent[s], "freq", ring(s)) for s in range(1, groups)]
    return turned


def gather(mine):
    other_core = [(0, 1), (1, 0), (2, 3), (3, 2)]
    other_y = [(0, 2), (2, 0), (1, 3), (3, 1)]
    place = lambda x, y, c: x * 4 + y * 2 + c
    far_y = lax.ppermute(mine, "col", other_y)
    columns = [
        lax.ppermute(
            mine,
            ("row", "col"),
            [(place(x, y, c), place(1 - x, x, y)) for x in range(2) for y in range(2)],
        )
        for c in range(2)
    ]
    near = lax.ppermute(mine, "col", other_core)
    far = lax.ppermute(far_y, "col", other_core)
    return [mine, near, far_y, far], columns


def fast(samples, input_gains, filter_taps):
    groups = lax.axis_size("freq")
    parts = PARTS
    half = SPEC // 2 // parts
    row_blocks, col_blocks = [], []
    for part in range(parts):
        sent = channelize(
            samples, input_gains, filter_taps, part * 2 * half, half, CUTS, groups
        )
        mine = regroup(exchange(sent, groups), half)
        rows, columns = gather(mine)
        row_blocks.append(rows)
        col_blocks.append(columns)
    return tuple(products(row_blocks, col_blocks, half))


PARTS = 1
CUTS = (0, 4, 8, 12, 16, 20, 24, 28, 32, 35)


def dft_table(channels):
    position = jnp.arange(NFFT, dtype=jnp.int32)
    channel = jnp.arange(channels, dtype=jnp.int32)
    phases = (position[:, None] * channel[None, :] % NFFT).astype(jnp.float32) * (
        2.0 * math.pi / NFFT
    )
    scaling = 0.5 / math.sqrt(NFFT)
    cosine = jnp.cos(phases) * scaling
    sine = jnp.sin(phases) * scaling
    real_rows = jnp.stack([cosine, -sine], axis=1)
    imag_rows = jnp.stack([sine, cosine], axis=1)
    return jnp.stack([real_rows, imag_rows], axis=0).astype(jnp.bfloat16)


def plain(samples, input_gains, filter_taps):
    channels = CH_DEV * lax.axis_size("freq")
    inputs_here = samples.shape[1]
    voltage = samples.astype(jnp.float32) * 0.25 * input_gains[None, :, None]
    frames = voltage.reshape(2, inputs_here, SPEC + TAPS - 1, NFFT)
    filtered = frames[:, :, 0:SPEC, :] * filter_taps[0]
    for tap_index in range(1, TAPS):
        filtered = filtered + frames[:, :, tap_index : tap_index + SPEC, :] * filter_taps[tap_index]
    filtered = filtered.astype(jnp.bfloat16)
    spectra = jnp.einsum(
        "pimn,pnqk->kiqm", filtered, dft_table(channels), preferred_element_type=jnp.float32
    )
    spectra = spectra.reshape(channels, inputs_here, 2 * SPEC).astype(jnp.bfloat16)
    grouped = lax.all_to_all(spectra, "freq", split_axis=0, concat_axis=1, tiled=True)
    row_count = lax.axis_size("row")
    column_count = lax.axis_size("col")
    everything = lax.all_gather(grouped, ("row", "col"), axis=1, tiled=True)
    row_size = everything.shape[1] // row_count
    column_size = everything.shape[1] // column_count
    row_data = lax.dynamic_slice_in_dim(everything, lax.axis_index("row") * row_size, row_size, 1)
    column_data = lax.dynamic_slice_in_dim(
        everything, lax.axis_index("col") * column_size, column_size, 1
    )
    rotated = jnp.concatenate([-column_data[:, :, SPEC:], column_data[:, :, :SPEC]], axis=2)
    stacked = jnp.concatenate([column_data, rotated], axis=1)
    product = jnp.einsum("kim,kjm->kij", row_data, stacked, preferred_element_type=jnp.float32) * (
        1.0 / SPEC
    )
    width = column_data.shape[1]
    vis_real = product[:, :, :width].astype(jnp.bfloat16)
    vis_imag = product[:, :, width:].astype(jnp.bfloat16)
    return (vis_real, vis_imag)


def solution(mesh):
    placed = (P(None, ("row", "col", "freq"), None), P(("row", "col", "freq")), P())
    fits = dict(mesh.shape) == {"freq": 4, "row": 2, "col": 4}
    return jax.shard_map(
        fast if fits else plain,
        mesh=mesh,
        in_specs=placed,
        out_specs=(P("freq", "row", "col"), P("freq", "row", "col")),
        check_vma=False,
    )
```

```python
import functools
import math

import jax
import jax.numpy as jnp
import numpy as np
from jax import lax
from jax.experimental import pallas as pl
from jax.experimental.pallas import tpu as pltpu
from jax.sharding import PartitionSpec as P

NFFT = 1024
TAPS = 4
SPEC = 64
CH_DEV = 4
LANES = 128
AHEAD = 3
VMEM_BYTES = 60 * 2**20


SHIFTS = (0, 2, 1, 3)


def partner(me, s, groups, sign=1):
    return lax.rem(me + sign * SHIFTS[s] + groups, groups)


def target_of(i, s, groups):
    return (i + SHIFTS[s]) % groups


def dft_rows(channels):
    phases = (np.arange(channels)[:, None] * np.arange(NFFT)[None, :] % NFFT) * (
        2.0 * math.pi / NFFT
    )
    scaling = 0.5 / math.sqrt(NFFT)
    cosine = np.cos(phases) * scaling
    sine = np.sin(phases) * scaling
    real_rows = np.concatenate([cosine, sine], axis=1)
    imag_rows = np.concatenate([-sine, cosine], axis=1)
    rows = np.stack([real_rows, imag_rows], axis=1).reshape(2 * channels, 2 * NFFT)
    return jnp.asarray(rows.astype(np.float32)).astype(jnp.bfloat16)


def channelize_body(
    gain_hbm, taps_hbm, table_hbm, samples_ref, *rest, first, half, blocks, groups
):
    outs, scratch = rest[:groups], rest[groups:]
    gain_ref, taps_ref, table_ref, weights, raw, lhs, sums, held, sems, small_sems = scratch
    inputs = samples_ref.shape[1]
    rows = table_ref.shape[0]
    small = [
        pltpu.make_async_copy(source, target, small_sems.at[index])
        for index, (source, target) in enumerate(
            [(taps_hbm, taps_ref), (table_hbm, table_ref), (gain_hbm, gain_ref)]
        )
    ]
    for copy in small:
        copy.start()
    copies = []
    for index, (start, stop) in enumerate(blocks):
        copies.append([])
        for side, begin, end in ((0, start, min(stop, half)), (1, half + start, half + stop)):
            if begin < end:
                span = pl.ds(begin * NFFT, (end - begin) * NFFT)
                source = pl.ds((first + begin) * NFFT, (end - begin) * NFFT)
                copy = pltpu.make_async_copy(
                    samples_ref.at[:, :, source], raw.at[:, :, span], sems.at[index, side]
                )
                copies[-1].append(copy)
    for index in range(min(AHEAD, len(blocks))):
        for copy in copies[index]:
            copy.start()
    for copy in small:
        copy.wait()
    for p in range(2):
        for b in range(NFFT // LANES):
            table = table_ref[:, p * NFFT + b * LANES : p * NFFT + (b + 1) * LANES].astype(
                jnp.float32
            )
            for t in range(TAPS):
                exact = table * taps_ref[t : t + 1, b * LANES : (b + 1) * LANES]
                high = exact.astype(jnp.bfloat16)
                low = (exact - high.astype(jnp.float32)).astype(jnp.bfloat16)
                at = pl.ds(p * NFFT + b * LANES, LANES)
                weights[t * rows : (t + 1) * rows, at] = high
                weights[(TAPS + t) * rows : (TAPS + t + 1) * rows, at] = low
    gain = gain_ref[...]
    gain = jnp.concatenate([gain, gain], axis=1) * (0.25 / math.sqrt(SPEC))
    for index, (start, stop) in enumerate(blocks):
        for copy in copies[index]:
            copy.wait()
        if index + AHEAD < len(blocks):
            for copy in copies[index + AHEAD]:
                copy.start()
        buffer = lhs[index % 2]
        for slot in range(start, stop):
            for side in range(2):
                frame = side * half + slot
                to = (slot - start) * 2 * inputs + side * inputs
                for p in range(2):
                    buffer[to : to + inputs, p * NFFT : (p + 1) * NFFT] = (
                        raw[p, :, frame * NFFT : (frame + 1) * NFFT]
                        .astype(jnp.float32)
                        .astype(jnp.bfloat16)
                    )
        size = (stop - start) * 2 * inputs
        both = lax.dot_general(
            weights[...],
            buffer[0:size, :],
            (((1,), (1,)), ((), ())),
            preferred_element_type=jnp.float32,
        )
        sums[:, start * LANES : stop * LANES] = both[: TAPS * rows] + both[TAPS * rows :]
        for slot in range(max(start - TAPS + 1, 0), stop - TAPS + 1):
            total = sums[0:rows, slot * LANES : (slot + 1) * LANES]
            for t in range(1, TAPS):
                total = total + sums[
                    t * rows : (t + 1) * rows, (slot + t) * LANES : (slot + t + 1) * LANES
                ]
            held[pl.ds(slot, rows, stride=half), :] = total * gain
    me = lax.axis_index("freq")
    depth = 2 * half
    for s in range(groups):
        to = partner(me, s, groups) * (CH_DEV * depth)
        for k in range(CH_DEV):
            outs[s][k] = held[
                pl.ds(pl.multiple_of(to + k * depth, 8), depth), :
            ].astype(jnp.bfloat16)


def channelize(samples, gains, taps, first, half, cuts, groups):
    inputs = samples.shape[1]
    channels = CH_DEV * groups
    rows = 2 * channels
    slots = half + TAPS - 1
    blocks = list(zip(cuts[:-1], cuts[1:]))
    widest = max(stop - start for start, stop in blocks)
    frames = 2 * half + TAPS - 1
    return pl.pallas_call(
        functools.partial(
            channelize_body, first=first, half=half, blocks=blocks, groups=groups
        ),
        in_specs=[pl.BlockSpec(memory_space=pltpu.HBM)] * 4,
        out_specs=[pl.BlockSpec(memory_space=pltpu.VMEM)] * groups,
        out_shape=[jax.ShapeDtypeStruct((CH_DEV, 2 * half, LANES), jnp.bfloat16)] * groups,
        scratch_shapes=[
            pltpu.VMEM((1, inputs), jnp.float32),
            pltpu.VMEM((TAPS, NFFT), jnp.float32),
            pltpu.VMEM((rows, 2 * NFFT), jnp.bfloat16),
            pltpu.VMEM((2 * TAPS * rows, 2 * NFFT), jnp.bfloat16),
            pltpu.VMEM((2, inputs, frames * NFFT), jnp.int32),
            [pltpu.VMEM((widest * 2 * inputs, 2 * NFFT), jnp.bfloat16)] * 2,
            pltpu.VMEM((TAPS * rows, slots * LANES), jnp.float32),
            pltpu.VMEM((rows * half, LANES), jnp.float32),
            pltpu.SemaphoreType.DMA((len(blocks), 2)),
            pltpu.SemaphoreType.DMA((3,)),
        ],
        compiler_params=pltpu.CompilerParams(vmem_limit_bytes=VMEM_BYTES),
        cost_estimate=pl.CostEstimate(
            flops=2 * 2 * NFFT * 256 * frames * inputs,
            bytes_accessed=8 * inputs * frames * NFFT,
            transcendentals=0,
        ),
        name="channelize",
    )(gains.reshape(1, inputs), taps, dft_rows(channels), samples)


def regroup_body(*refs, half):
    groups = len(refs) - 2
    sources, out, ordered = refs[:groups], refs[groups], refs[groups + 1]
    me = lax.axis_index("freq")
    for s in range(groups):
        ordered[partner(me, s, groups, -1)] = sources[s][...]
    depth = 2 * half
    lane = lax.broadcasted_iota(jnp.int32, (depth, LANES), 1)
    for pair in range(groups // 2):
        for k in range(CH_DEV):
            left = ordered[2 * pair, k].astype(jnp.float32)
            right = ordered[2 * pair + 1, k].astype(jnp.float32)
            early = jnp.where(lane < LANES // 2, left, pltpu.roll(right, LANES // 2, 1))
            late = jnp.where(lane < LANES // 2, pltpu.roll(left, LANES // 2, 1), right)
            at = pl.ds(pair * LANES, LANES)
            out[k, 0:depth, at] = early.astype(jnp.bfloat16)
            out[k, depth : 2 * depth, at] = late.astype(jnp.bfloat16)


def regroup(sources, half):
    groups = len(sources)
    shape = (CH_DEV, 4 * half, groups * LANES // 2)
    return pl.pallas_call(
        functools.partial(regroup_body, half=half),
        out_shape=jax.ShapeDtypeStruct(shape, jnp.bfloat16),
        scratch_shapes=[pltpu.VMEM((groups,) + sources[0].shape, jnp.bfloat16)],
        compiler_params=pltpu.CompilerParams(vmem_limit_bytes=4 * 2**20),
        name="regroup",
    )(*sources)


def products_body(*refs, half, parts):
    rows_in = [refs[4 * part : 4 * part + 4] for part in range(parts)]
    cols_in = [refs[4 * parts + 2 * part : 4 * parts + 2 * part + 2] for part in range(parts)]
    real, imag, left, right = refs[6 * parts :]
    row, col = lax.axis_index("row"), lax.axis_index("col")
    y, core = col // 2, lax.rem(col, 2)
    width = rows_in[0][0].shape[2]
    deep = 4 * half
    for part in range(parts):
        down = slice(part * deep, (part + 1) * deep)
        for flip_y in range(2):
            for flip_core in range(2):
                block = (y + flip_y) % 2 * 2 + (core + flip_core) % 2
                left[block, down, :] = rows_in[part][2 * flip_y + flip_core][0]
    for t in range(2):
        across = slice(t * width, (t + 1) * width)

        @pl.when(row == y)
        def _():
            right[:, across] = left[core * 2 + t]

        @pl.when(row != y)
        def _():
            for part in range(parts):
                down = slice(part * deep, (part + 1) * deep)
                right[down, across] = cols_in[part][t][0]

    columns = 2 * width
    for at in range(0, parts * deep, 2 * half):
        re, im = right[at : at + half, 0:columns], right[at + half : at + 2 * half, 0:columns]
        right[at : at + half, columns : 2 * columns] = -im
        right[at + half : at + 2 * half, columns : 2 * columns] = re
    for block in range(4):
        product = lax.dot_general(
            left[block],
            right[...],
            (((0,), (0,)), ((), ())),
            preferred_element_type=jnp.float32,
        )
        at = slice(block * width, (block + 1) * width)
        real[0, at, :] = product[:, 0:columns].astype(jnp.bfloat16)
        imag[0, at, :] = product[:, columns : 2 * columns].astype(jnp.bfloat16)


def products(row_blocks, col_blocks, half):
    parts = len(row_blocks)
    _, deep, width = row_blocks[0][0].shape
    flat = [a for part in row_blocks for a in part] + [a for part in col_blocks for a in part]
    out = jax.ShapeDtypeStruct((CH_DEV, 4 * width, 2 * width), jnp.bfloat16)
    return pl.pallas_call(
        functools.partial(products_body, half=half, parts=parts),
        grid=(CH_DEV,),
        in_specs=[pl.BlockSpec((1, deep, width), lambda k: (k, 0, 0))] * len(flat),
        out_specs=[pl.BlockSpec((1, 4 * width, 2 * width), lambda k: (k, 0, 0))] * 2,
        out_shape=[out, out],
        scratch_shapes=[
            pltpu.VMEM((4, parts * deep, width), jnp.bfloat16),
            pltpu.VMEM((parts * deep, 4 * width), jnp.bfloat16),
        ],
        compiler_params=pltpu.CompilerParams(vmem_limit_bytes=24 * 2**20),
        cost_estimate=pl.CostEstimate(
            flops=2 * CH_DEV * parts * deep * 16 * width * width,
            bytes_accessed=2 * 2 * CH_DEV * 8 * width * width,
            transcendentals=0,
        ),
        name="products",
    )(*flat)


def exchange(sent, groups):
    moves = [[(i, target_of(i, s, groups)) for i in range(groups)] for s in range(groups)]
    return [sent[0]] + [lax.ppermute(sent[s], "freq", moves[s]) for s in range(1, groups)]


def gather(mine):
    other_core = [(0, 1), (1, 0), (2, 3), (3, 2)]
    other_y = [(0, 2), (2, 0), (1, 3), (3, 1)]
    place = lambda x, y, c: x * 4 + y * 2 + c
    far_y = lax.ppermute(mine, "col", other_y)
    columns = [
        lax.ppermute(
            mine,
            ("row", "col"),
            [(place(x, y, c), place(1 - x, x, y)) for x in range(2) for y in range(2)],
        )
        for c in range(2)
    ]
    near = lax.ppermute(mine, "col", other_core)
    far = lax.ppermute(far_y, "col", other_core)
    return [mine, near, far_y, far], columns


def fast(samples, input_gains, filter_taps):
    groups = lax.axis_size("freq")
    parts = PARTS
    half = SPEC // 2 // parts
    row_blocks, col_blocks = [], []
    for part in range(parts):
        sent = channelize(
            samples, input_gains, filter_taps, part * 2 * half, half, CUTS, groups
        )
        mine = regroup(exchange(sent, groups), half)
        rows, columns = gather(mine)
        row_blocks.append(rows)
        col_blocks.append(columns)
    return tuple(products(row_blocks, col_blocks, half))


PARTS = 1
CUTS = (0, 4, 8, 12, 16, 20, 24, 28, 32, 35)


def dft_table(channels):
    position = jnp.arange(NFFT, dtype=jnp.int32)
    channel = jnp.arange(channels, dtype=jnp.int32)
    phases = (position[:, None] * channel[None, :] % NFFT).astype(jnp.float32) * (
        2.0 * math.pi / NFFT
    )
    scaling = 0.5 / math.sqrt(NFFT)
    cosine = jnp.cos(phases) * scaling
    sine = jnp.sin(phases) * scaling
    real_rows = jnp.stack([cosine, -sine], axis=1)
    imag_rows = jnp.stack([sine, cosine], axis=1)
    return jnp.stack([real_rows, imag_rows], axis=0).astype(jnp.bfloat16)


def plain(samples, input_gains, filter_taps):
    channels = CH_DEV * lax.axis_size("freq")
    inputs_here = samples.shape[1]
    voltage = samples.astype(jnp.float32) * 0.25 * input_gains[None, :, None]
    frames = voltage.reshape(2, inputs_here, SPEC + TAPS - 1, NFFT)
    filtered = frames[:, :, 0:SPEC, :] * filter_taps[0]
    for tap_index in range(1, TAPS):
        filtered = filtered + frames[:, :, tap_index : tap_index + SPEC, :] * filter_taps[tap_index]
    filtered = filtered.astype(jnp.bfloat16)
    spectra = jnp.einsum(
        "pimn,pnqk->kiqm", filtered, dft_table(channels), preferred_element_type=jnp.float32
    )
    spectra = spectra.reshape(channels, inputs_here, 2 * SPEC).astype(jnp.bfloat16)
    grouped = lax.all_to_all(spectra, "freq", split_axis=0, concat_axis=1, tiled=True)
    row_count = lax.axis_size("row")
    column_count = lax.axis_size("col")
    everything = lax.all_gather(grouped, ("row", "col"), axis=1, tiled=True)
    row_size = everything.shape[1] // row_count
    column_size = everything.shape[1] // column_count
    row_data = lax.dynamic_slice_in_dim(everything, lax.axis_index("row") * row_size, row_size, 1)
    column_data = lax.dynamic_slice_in_dim(
        everything, lax.axis_index("col") * column_size, column_size, 1
    )
    rotated = jnp.concatenate([-column_data[:, :, SPEC:], column_data[:, :, :SPEC]], axis=2)
    stacked = jnp.concatenate([column_data, rotated], axis=1)
    product = jnp.einsum("kim,kjm->kij", row_data, stacked, preferred_element_type=jnp.float32) * (
        1.0 / SPEC
    )
    width = column_data.shape[1]
    vis_real = product[:, :, :width].astype(jnp.bfloat16)
    vis_imag = product[:, :, width:].astype(jnp.bfloat16)
    return (vis_real, vis_imag)


def solution(mesh):
    placed = (P(None, ("row", "col", "freq"), None), P(("row", "col", "freq")), P())
    fits = dict(mesh.shape) == {"freq": 4, "row": 2, "col": 4}
    return jax.shard_map(
        fast if fits else plain,
        mesh=mesh,
        in_specs=placed,
        out_specs=(P("freq", "row", "col"), P("freq", "row", "col")),
        check_vma=False,
    )
```

```python
import functools
import math

import jax
import jax.numpy as jnp
import numpy as np
from jax import lax
from jax.experimental import pallas as pl
from jax.experimental.pallas import tpu as pltpu
from jax.sharding import PartitionSpec as P

NFFT = 1024
TAPS = 4
SPEC = 64
CH_DEV = 4
LANES = 128
AHEAD = 3
VMEM_BYTES = 60 * 2**20


SHIFTS = (0, 2, 1, 3)


def partner(me, s, groups, sign=1):
    return lax.rem(me + sign * SHIFTS[s] + groups, groups)


def target_of(i, s, groups):
    return (i + SHIFTS[s]) % groups


def dft_rows(channels):
    phases = (np.arange(channels)[:, None] * np.arange(NFFT)[None, :] % NFFT) * (
        2.0 * math.pi / NFFT
    )
    scaling = 0.5 / math.sqrt(NFFT)
    cosine = np.cos(phases) * scaling
    sine = np.sin(phases) * scaling
    real_rows = np.concatenate([cosine, sine], axis=1)
    imag_rows = np.concatenate([-sine, cosine], axis=1)
    rows = np.stack([real_rows, imag_rows], axis=1).reshape(2 * channels, 2 * NFFT)
    return jnp.asarray(rows.astype(np.float32)).astype(jnp.bfloat16)


def channelize_body(
    gain_hbm, taps_hbm, table_hbm, samples_ref, *rest, first, half, blocks, groups
):
    outs, scratch = rest[:groups], rest[groups:]
    gain_ref, taps_ref, table_ref, weights, raw, lhs, sums, held, sems, small_sems = scratch
    inputs = samples_ref.shape[1]
    rows = table_ref.shape[0]
    small = [
        pltpu.make_async_copy(source, target, small_sems.at[index])
        for index, (source, target) in enumerate(
            [(taps_hbm, taps_ref), (table_hbm, table_ref), (gain_hbm, gain_ref)]
        )
    ]
    for copy in small:
        copy.start()
    copies = []
    for index, (start, stop) in enumerate(blocks):
        copies.append([])
        for side, begin, end in ((0, start, min(stop, half)), (1, half + start, half + stop)):
            if begin < end:
                span = pl.ds(begin * NFFT, (end - begin) * NFFT)
                source = pl.ds((first + begin) * NFFT, (end - begin) * NFFT)
                copy = pltpu.make_async_copy(
                    samples_ref.at[:, :, source], raw.at[:, :, span], sems.at[index, side]
                )
                copies[-1].append(copy)
    for index in range(min(AHEAD, len(blocks))):
        for copy in copies[index]:
            copy.start()
    for copy in small:
        copy.wait()
    for p in range(2):
        for b in range(NFFT // LANES):
            table = table_ref[:, p * NFFT + b * LANES : p * NFFT + (b + 1) * LANES].astype(
                jnp.float32
            )
            for t in range(TAPS):
                exact = table * taps_ref[t : t + 1, b * LANES : (b + 1) * LANES]
                high = exact.astype(jnp.bfloat16)
                low = (exact - high.astype(jnp.float32)).astype(jnp.bfloat16)
                at = pl.ds(p * NFFT + b * LANES, LANES)
                weights[t * rows : (t + 1) * rows, at] = high
                weights[(TAPS + t) * rows : (TAPS + t + 1) * rows, at] = low
    gain = gain_ref[...]
    gain = jnp.concatenate([gain, gain], axis=1) * (0.25 / math.sqrt(SPEC))
    for index, (start, stop) in enumerate(blocks):
        for copy in copies[index]:
            copy.wait()
        if index + AHEAD < len(blocks):
            for copy in copies[index + AHEAD]:
                copy.start()
        buffer = lhs[index % 2]
        for slot in range(start, stop):
            for side in range(2):
                frame = side * half + slot
                to = (slot - start) * 2 * inputs + side * inputs
                for p in range(2):
                    buffer[to : to + inputs, p * NFFT : (p + 1) * NFFT] = (
                        raw[p, :, frame * NFFT : (frame + 1) * NFFT]
                        .astype(jnp.float32)
                        .astype(jnp.bfloat16)
                    )
        size = (stop - start) * 2 * inputs
        both = lax.dot_general(
            weights[...],
            buffer[0:size, :],
            (((1,), (1,)), ((), ())),
            preferred_element_type=jnp.float32,
        )
        sums[:, start * LANES : stop * LANES] = both[: TAPS * rows] + both[TAPS * rows :]
        for slot in range(max(start - TAPS + 1, 0), stop - TAPS + 1):
            total = sums[0:rows, slot * LANES : (slot + 1) * LANES]
            for t in range(1, TAPS):
                total = total + sums[
                    t * rows : (t + 1) * rows, (slot + t) * LANES : (slot + t + 1) * LANES
                ]
            held[pl.ds(slot, rows, stride=half), :] = total * gain
    me = lax.axis_index("freq")
    depth = 2 * half
    for s in range(groups):
        to = partner(me, s, groups) * (CH_DEV * depth)
        for k in range(CH_DEV):
            outs[s][k] = held[
                pl.ds(pl.multiple_of(to + k * depth, 8), depth), :
            ].astype(jnp.bfloat16)


def channelize(samples, gains, taps, first, half, cuts, groups):
    inputs = samples.shape[1]
    channels = CH_DEV * groups
    rows = 2 * channels
    slots = half + TAPS - 1
    blocks = list(zip(cuts[:-1], cuts[1:]))
    widest = max(stop - start for start, stop in blocks)
    frames = 2 * half + TAPS - 1
    return pl.pallas_call(
        functools.partial(
            channelize_body, first=first, half=half, blocks=blocks, groups=groups
        ),
        in_specs=[pl.BlockSpec(memory_space=pltpu.HBM)] * 4,
        out_specs=[pl.BlockSpec(memory_space=pltpu.VMEM)] * groups,
        out_shape=[jax.ShapeDtypeStruct((CH_DEV, 2 * half, LANES), jnp.bfloat16)] * groups,
        scratch_shapes=[
            pltpu.VMEM((1, inputs), jnp.float32),
            pltpu.VMEM((TAPS, NFFT), jnp.float32),
            pltpu.VMEM((rows, 2 * NFFT), jnp.bfloat16),
            pltpu.VMEM((2 * TAPS * rows, 2 * NFFT), jnp.bfloat16),
            pltpu.VMEM((2, inputs, frames * NFFT), jnp.int32),
            [pltpu.VMEM((widest * 2 * inputs, 2 * NFFT), jnp.bfloat16)] * 2,
            pltpu.VMEM((TAPS * rows, slots * LANES), jnp.float32),
            pltpu.VMEM((rows * half, LANES), jnp.float32),
            pltpu.SemaphoreType.DMA((len(blocks), 2)),
            pltpu.SemaphoreType.DMA((3,)),
        ],
        compiler_params=pltpu.CompilerParams(vmem_limit_bytes=VMEM_BYTES),
        cost_estimate=pl.CostEstimate(
            flops=2 * 2 * NFFT * 256 * frames * inputs,
            bytes_accessed=8 * inputs * frames * NFFT,
            transcendentals=0,
        ),
        name="channelize",
    )(gains.reshape(1, inputs), taps, dft_rows(channels), samples)


def hold_body(source, out):
    out[...] = source[...]


def hold(array):
    return pl.pallas_call(
        hold_body,
        out_shape=jax.ShapeDtypeStruct(array.shape, array.dtype),
        in_specs=[pl.BlockSpec(memory_space=pltpu.VMEM)],
        out_specs=pl.BlockSpec(memory_space=pltpu.VMEM),
        compiler_params=pltpu.CompilerParams(vmem_limit_bytes=2 * 2**20),
        cost_estimate=pl.CostEstimate(flops=4 * 10**10, bytes_accessed=0, transcendentals=0),
        name="hold",
    )(array)


def regroup_body(*refs, half):
    groups = len(refs) - 2
    sources, out, ordered = refs[:groups], refs[groups], refs[groups + 1]
    me = lax.axis_index("freq")
    for s in range(groups):
        ordered[partner(me, s, groups, -1)] = sources[s][...]
    depth = 2 * half
    lane = lax.broadcasted_iota(jnp.int32, (depth, LANES), 1)
    for pair in range(groups // 2):
        for k in range(CH_DEV):
            left = ordered[2 * pair, k].astype(jnp.float32)
            right = ordered[2 * pair + 1, k].astype(jnp.float32)
            early = jnp.where(lane < LANES // 2, left, pltpu.roll(right, LANES // 2, 1))
            late = jnp.where(lane < LANES // 2, pltpu.roll(left, LANES // 2, 1), right)
            at = pl.ds(pair * LANES, LANES)
            out[k, 0:depth, at] = early.astype(jnp.bfloat16)
            out[k, depth : 2 * depth, at] = late.astype(jnp.bfloat16)


def regroup(sources, half):
    groups = len(sources)
    shape = (CH_DEV, 4 * half, groups * LANES // 2)
    return pl.pallas_call(
        functools.partial(regroup_body, half=half),
        out_shape=jax.ShapeDtypeStruct(shape, jnp.bfloat16),
        scratch_shapes=[pltpu.VMEM((groups,) + sources[0].shape, jnp.bfloat16)],
        compiler_params=pltpu.CompilerParams(vmem_limit_bytes=4 * 2**20),
        name="regroup",
    )(*sources)


def products_body(*refs, half):
    rows_in, cols_in = refs[0:4], refs[4:6]
    outs, right, staged, sems = refs[6:8], refs[8], refs[9:11], refs[11]
    row, col = lax.axis_index("row"), lax.axis_index("col")
    y, core = col // 2, lax.rem(col, 2)
    deep, width = rows_in[0].shape[1:]
    columns = 2 * width
    copies = []
    for k in range(CH_DEV):
        for flip_y in range(2):

            @pl.when((row == y) & ((core != y) if flip_y else (core == y)))
            def _():
                for flip_core in range(2):
                    at = pl.multiple_of(lax.rem(core + flip_core, 2) * width, width)
                    right[k, :, pl.ds(at, width)] = rows_in[2 * flip_y + flip_core][k]

        @pl.when(row != y)
        def _():
            for t in range(2):
                right[k, :, t * width : (t + 1) * width] = cols_in[t][k]

        for at in range(0, deep, 2 * half):
            re = right[k, at : at + half, 0:columns]
            im = right[k, at + half : at + 2 * half, 0:columns]
            right[k, at : at + half, columns : 2 * columns] = -im
            right[k, at + half : at + 2 * half, columns : 2 * columns] = re
        for begin in range(0, 4, TOGETHER):
            sources = range(begin, begin + TOGETHER)
            product = lax.dot_general(
                jnp.concatenate([rows_in[source][k] for source in sources], axis=1),
                right[k],
                (((0,), (0,)), ((), ())),
                preferred_element_type=jnp.float32,
            )
            for source in sources:
                from_row = (source - begin) * width
                block = lax.rem(y + source // 2, 2) * 2 + lax.rem(core + source % 2, 2)
                to = pl.ds(pl.multiple_of(block * width, width), width)
                for q in range(2):
                    staged[q][k, source * width : (source + 1) * width, :] = product[
                        from_row : from_row + width, q * columns : (q + 1) * columns
                    ].astype(jnp.bfloat16)
                    copy = pltpu.make_async_copy(
                        staged[q].at[k, pl.ds(source * width, width), :],
                        outs[q].at[k, to, :],
                        sems.at[k, source, q],
                    )
                    copy.start()
                    copies.append(copy)
    for copy in copies:
        copy.wait()


def products(row_blocks, col_blocks, half):
    _, deep, width = row_blocks[0][0].shape
    flat = [a for part in row_blocks for a in part] + [a for part in col_blocks for a in part]
    shape = (CH_DEV, 4 * width, 2 * width)
    out = jax.ShapeDtypeStruct(shape, jnp.bfloat16)
    return pl.pallas_call(
        functools.partial(products_body, half=half),
        in_specs=[pl.BlockSpec(memory_space=pltpu.VMEM)] * len(flat),
        out_specs=[pl.BlockSpec(memory_space=pltpu.HBM)] * 2,
        out_shape=[out, out],
        scratch_shapes=[
            pltpu.VMEM((CH_DEV, deep, 4 * width), jnp.bfloat16),
            pltpu.VMEM(shape, jnp.bfloat16),
            pltpu.VMEM(shape, jnp.bfloat16),
            pltpu.SemaphoreType.DMA((CH_DEV, 4, 2)),
        ],
        compiler_params=pltpu.CompilerParams(vmem_limit_bytes=28 * 2**20),
        cost_estimate=pl.CostEstimate(
            flops=2 * CH_DEV * deep * 16 * width * width,
            bytes_accessed=2 * 2 * CH_DEV * 8 * width * width,
            transcendentals=0,
        ),
        name="products",
    )(*flat)


TOGETHER = 1


def exchange(sent, groups):
    moves = [[(i, target_of(i, s, groups)) for i in range(groups)] for s in range(groups)]
    return [sent[0]] + [lax.ppermute(sent[s], "freq", moves[s]) for s in range(1, groups)]


def gather(mine):
    other_core = [(0, 1), (1, 0), (2, 3), (3, 2)]
    other_y = [(0, 2), (2, 0), (1, 3), (3, 1)]
    place = lambda x, y, c: x * 4 + y * 2 + c
    far_y = lax.ppermute(mine, "col", other_y)
    columns = [
        lax.ppermute(
            mine,
            ("row", "col"),
            [(place(x, y, c), place(1 - x, x, y)) for x in range(2) for y in range(2)],
        )
        for c in range(2)
    ]
    near = lax.ppermute(mine, "col", other_core)
    far = lax.ppermute(far_y, "col", other_core)
    return [mine, near, far_y, far], columns


def fast(samples, input_gains, filter_taps):
    groups = lax.axis_size("freq")
    parts = PARTS
    half = SPEC // 2 // parts
    row_blocks, col_blocks = [], []
    for part in range(parts):
        sent = channelize(
            samples, input_gains, filter_taps, part * 2 * half, half, CUTS, groups
        )
        turned = exchange(sent, groups)
        turned[1] = hold(turned[1])
        mine = regroup(turned, half)
        rows, columns = gather(mine)
        row_blocks.append(rows)
        col_blocks.append(columns)
    return tuple(products(row_blocks, col_blocks, half))


PARTS = 1
CUTS = (0, 4, 8, 12, 16, 20, 24, 28, 32, 35)


def dft_table(channels):
    position = jnp.arange(NFFT, dtype=jnp.int32)
    channel = jnp.arange(channels, dtype=jnp.int32)
    phases = (position[:, None] * channel[None, :] % NFFT).astype(jnp.float32) * (
        2.0 * math.pi / NFFT
    )
    scaling = 0.5 / math.sqrt(NFFT)
    cosine = jnp.cos(phases) * scaling
    sine = jnp.sin(phases) * scaling
    real_rows = jnp.stack([cosine, -sine], axis=1)
    imag_rows = jnp.stack([sine, cosine], axis=1)
    return jnp.stack([real_rows, imag_rows], axis=0).astype(jnp.bfloat16)


def plain(samples, input_gains, filter_taps):
    channels = CH_DEV * lax.axis_size("freq")
    inputs_here = samples.shape[1]
    voltage = samples.astype(jnp.float32) * 0.25 * input_gains[None, :, None]
    frames = voltage.reshape(2, inputs_here, SPEC + TAPS - 1, NFFT)
    filtered = frames[:, :, 0:SPEC, :] * filter_taps[0]
    for tap_index in range(1, TAPS):
        filtered = filtered + frames[:, :, tap_index : tap_index + SPEC, :] * filter_taps[tap_index]
    filtered = filtered.astype(jnp.bfloat16)
    spectra = jnp.einsum(
        "pimn,pnqk->kiqm", filtered, dft_table(channels), preferred_element_type=jnp.float32
    )
    spectra = spectra.reshape(channels, inputs_here, 2 * SPEC).astype(jnp.bfloat16)
    grouped = lax.all_to_all(spectra, "freq", split_axis=0, concat_axis=1, tiled=True)
    row_count = lax.axis_size("row")
    column_count = lax.axis_size("col")
    everything = lax.all_gather(grouped, ("row", "col"), axis=1, tiled=True)
    row_size = everything.shape[1] // row_count
    column_size = everything.shape[1] // column_count
    row_data = lax.dynamic_slice_in_dim(everything, lax.axis_index("row") * row_size, row_size, 1)
    column_data = lax.dynamic_slice_in_dim(
        everything, lax.axis_index("col") * column_size, column_size, 1
    )
    rotated = jnp.concatenate([-column_data[:, :, SPEC:], column_data[:, :, :SPEC]], axis=2)
    stacked = jnp.concatenate([column_data, rotated], axis=1)
    product = jnp.einsum("kim,kjm->kij", row_data, stacked, preferred_element_type=jnp.float32) * (
        1.0 / SPEC
    )
    width = column_data.shape[1]
    vis_real = product[:, :, :width].astype(jnp.bfloat16)
    vis_imag = product[:, :, width:].astype(jnp.bfloat16)
    return (vis_real, vis_imag)


def solution(mesh):
    placed = (P(None, ("row", "col", "freq"), None), P(("row", "col", "freq")), P())
    fits = dict(mesh.shape) == {"freq": 4, "row": 2, "col": 4}
    return jax.shard_map(
        fast if fits else plain,
        mesh=mesh,
        in_specs=placed,
        out_specs=(P("freq", "row", "col"), P("freq", "row", "col")),
        check_vma=False,
    )
```

```python
import functools
import math

import jax
import jax.numpy as jnp
import numpy as np
from jax import lax
from jax.experimental import pallas as pl
from jax.experimental.pallas import tpu as pltpu
from jax.sharding import PartitionSpec as P

NFFT = 1024
TAPS = 4
SPEC = 64
CH_DEV = 4
LANES = 128
AHEAD = 2
VMEM_BYTES = 60 * 2**20


SHIFTS = (0, 2, 1, 3)


def partner(me, s, groups, sign=1):
    return lax.rem(me + sign * SHIFTS[s] + groups, groups)


def target_of(i, s, groups):
    return (i + SHIFTS[s]) % groups


def dft_rows(channels):
    phases = (np.arange(channels)[:, None] * np.arange(NFFT)[None, :] % NFFT) * (
        2.0 * math.pi / NFFT
    )
    scaling = 0.5 / math.sqrt(NFFT)
    cosine = np.cos(phases) * scaling
    sine = np.sin(phases) * scaling
    real_rows = np.concatenate([cosine, sine], axis=1)
    imag_rows = np.concatenate([-sine, cosine], axis=1)
    rows = np.stack([real_rows, imag_rows], axis=1).reshape(2 * channels, 2 * NFFT)
    return jnp.asarray(rows.astype(np.float32)).astype(jnp.bfloat16)


def channelize_body(
    gain_hbm, taps_hbm, table_hbm, samples_ref, *rest, first, half, blocks, groups
):
    outs, scratch = rest[:groups], rest[groups:]
    gain_ref, taps_ref, table_ref, weights, raw, lhs, sums, held, staged = scratch[:9]
    sems, small_sems, out_sems = scratch[9:]
    inputs = samples_ref.shape[1]
    rows = table_ref.shape[0]
    small = [
        pltpu.make_async_copy(source, target, small_sems.at[index])
        for index, (source, target) in enumerate(
            [(taps_hbm, taps_ref), (table_hbm, table_ref), (gain_hbm, gain_ref)]
        )
    ]
    for copy in small:
        copy.start()
    copies = []
    for index, (start, stop) in enumerate(blocks):
        copies.append([])
        for side, begin, end in ((0, start, min(stop, half)), (1, half + start, half + stop)):
            if begin < end:
                span = pl.ds(begin * NFFT, (end - begin) * NFFT)
                source = pl.ds((first + begin) * NFFT, (end - begin) * NFFT)
                copy = pltpu.make_async_copy(
                    samples_ref.at[:, :, source], raw.at[:, :, span], sems.at[index, side]
                )
                copies[-1].append(copy)
    for index in range(min(AHEAD, len(blocks))):
        for copy in copies[index]:
            copy.start()
    for copy in small:
        copy.wait()
    for index in range(AHEAD, len(blocks)):
        for copy in copies[index]:
            copy.start()
    for p in range(2):
        for b in range(NFFT // LANES):
            table = table_ref[:, p * NFFT + b * LANES : p * NFFT + (b + 1) * LANES].astype(
                jnp.float32
            )
            for t in range(TAPS):
                exact = table * taps_ref[t : t + 1, b * LANES : (b + 1) * LANES]
                high = exact.astype(jnp.bfloat16)
                low = (exact - high.astype(jnp.float32)).astype(jnp.bfloat16)
                at = pl.ds(p * NFFT + b * LANES, LANES)
                weights[t * rows : (t + 1) * rows, at] = high
                weights[(TAPS + t) * rows : (TAPS + t + 1) * rows, at] = low
    gain = gain_ref[...]
    gain = jnp.concatenate([gain, gain], axis=1) * (0.25 / math.sqrt(SPEC))
    for index, (start, stop) in enumerate(blocks):
        for copy in copies[index]:
            copy.wait()
        buffer = lhs[index % 2]
        for slot in range(start, stop):
            for side in range(2):
                frame = side * half + slot
                to = (slot - start) * 2 * inputs + side * inputs
                for p in range(2):
                    buffer[to : to + inputs, p * NFFT : (p + 1) * NFFT] = (
                        raw[p, :, frame * NFFT : (frame + 1) * NFFT]
                        .astype(jnp.float32)
                        .astype(jnp.bfloat16)
                    )
        size = (stop - start) * 2 * inputs
        both = lax.dot_general(
            weights[...],
            buffer[0:size, :],
            (((1,), (1,)), ((), ())),
            preferred_element_type=jnp.float32,
        )
        sums[:, start * LANES : stop * LANES] = both[: TAPS * rows] + both[TAPS * rows :]
        for slot in range(max(start - TAPS + 1, 0), stop - TAPS + 1):
            total = sums[0:rows, slot * LANES : (slot + 1) * LANES]
            for t in range(1, TAPS):
                total = total + sums[
                    t * rows : (t + 1) * rows, (slot + t) * LANES : (slot + t + 1) * LANES
                ]
            held[pl.ds(slot, rows, stride=half), :] = total * gain
    me = lax.axis_index("freq")
    depth = 2 * half
    sent = []
    for s in range(groups):
        to = partner(me, s, groups) * (CH_DEV * depth)
        for k in range(CH_DEV):
            staged[s, k] = held[
                pl.ds(pl.multiple_of(to + k * depth, 8), depth), :
            ].astype(jnp.bfloat16)
        sent.append(pltpu.make_async_copy(staged.at[s], outs[s], out_sems.at[s]))
        sent[-1].start()
    for copy in sent:
        copy.wait()


def channelize(samples, gains, taps, first, half, cuts, groups):
    inputs = samples.shape[1]
    channels = CH_DEV * groups
    rows = 2 * channels
    slots = half + TAPS - 1
    blocks = list(zip(cuts[:-1], cuts[1:]))
    widest = max(stop - start for start, stop in blocks)
    frames = 2 * half + TAPS - 1
    return pl.pallas_call(
        functools.partial(
            channelize_body, first=first, half=half, blocks=blocks, groups=groups
        ),
        in_specs=[pl.BlockSpec(memory_space=pltpu.HBM)] * 4,
        out_specs=[pl.BlockSpec(memory_space=pltpu.HBM)] * groups,
        out_shape=[jax.ShapeDtypeStruct((CH_DEV, 2 * half, LANES), jnp.bfloat16)] * groups,
        scratch_shapes=[
            pltpu.VMEM((1, inputs), jnp.float32),
            pltpu.VMEM((TAPS, NFFT), jnp.float32),
            pltpu.VMEM((rows, 2 * NFFT), jnp.bfloat16),
            pltpu.VMEM((2 * TAPS * rows, 2 * NFFT), jnp.bfloat16),
            pltpu.VMEM((2, inputs, frames * NFFT), jnp.int32),
            [pltpu.VMEM((widest * 2 * inputs, 2 * NFFT), jnp.bfloat16)] * 2,
            pltpu.VMEM((TAPS * rows, slots * LANES), jnp.float32),
            pltpu.VMEM((rows * half, LANES), jnp.float32),
            pltpu.VMEM((groups, CH_DEV, 2 * half, LANES), jnp.bfloat16),
            pltpu.SemaphoreType.DMA((len(blocks), 2)),
            pltpu.SemaphoreType.DMA((3,)),
            pltpu.SemaphoreType.DMA((groups,)),
        ],
        compiler_params=pltpu.CompilerParams(vmem_limit_bytes=VMEM_BYTES),
        cost_estimate=pl.CostEstimate(
            flops=2 * 2 * NFFT * 256 * frames * inputs,
            bytes_accessed=8 * inputs * frames * NFFT,
            transcendentals=0,
        ),
        name="channelize",
    )(gains.reshape(1, inputs), taps, dft_rows(channels), samples)


def hold_body(source, out):
    out[...] = source[...]


def hold(array):
    return pl.pallas_call(
        hold_body,
        out_shape=jax.ShapeDtypeStruct(array.shape, array.dtype),
        in_specs=[pl.BlockSpec(memory_space=pltpu.VMEM)],
        out_specs=pl.BlockSpec(memory_space=pltpu.VMEM),
        compiler_params=pltpu.CompilerParams(vmem_limit_bytes=2 * 2**20),
        cost_estimate=pl.CostEstimate(flops=4 * 10**10, bytes_accessed=0, transcendentals=0),
        name="hold",
    )(array)


def regroup_body(*refs, half):
    groups = len(refs) - 2
    sources, out, ordered = refs[:groups], refs[groups], refs[groups + 1]
    me = lax.axis_index("freq")
    for s in range(groups):
        ordered[partner(me, s, groups, -1)] = sources[s][...]
    depth = 2 * half
    lane = lax.broadcasted_iota(jnp.int32, (depth, LANES), 1)
    for pair in range(groups // 2):
        for k in range(CH_DEV):
            left = ordered[2 * pair, k].astype(jnp.float32)
            right = ordered[2 * pair + 1, k].astype(jnp.float32)
            early = jnp.where(lane < LANES // 2, left, pltpu.roll(right, LANES // 2, 1))
            late = jnp.where(lane < LANES // 2, pltpu.roll(left, LANES // 2, 1), right)
            at = pl.ds(pair * LANES, LANES)
            out[k, 0:depth, at] = early.astype(jnp.bfloat16)
            out[k, depth : 2 * depth, at] = late.astype(jnp.bfloat16)


def regroup(sources, half):
    groups = len(sources)
    shape = (CH_DEV, 4 * half, groups * LANES // 2)
    return pl.pallas_call(
        functools.partial(regroup_body, half=half),
        out_shape=jax.ShapeDtypeStruct(shape, jnp.bfloat16),
        scratch_shapes=[pltpu.VMEM((groups,) + sources[0].shape, jnp.bfloat16)],
        compiler_params=pltpu.CompilerParams(vmem_limit_bytes=4 * 2**20),
        name="regroup",
    )(*sources)


def products_body(*refs, half):
    rows_in, cols_in = refs[0:4], refs[4:6]
    outs, right, staged, sems = refs[6:8], refs[8], refs[9:11], refs[11]
    row, col = lax.axis_index("row"), lax.axis_index("col")
    y, core = col // 2, lax.rem(col, 2)
    deep, width = rows_in[0].shape[1:]
    columns = 2 * width
    copies = []
    for k in range(CH_DEV):
        for flip_y in range(2):

            @pl.when((row == y) & ((core != y) if flip_y else (core == y)))
            def _():
                for flip_core in range(2):
                    at = pl.multiple_of(lax.rem(core + flip_core, 2) * width, width)
                    right[k, :, pl.ds(at, width)] = rows_in[2 * flip_y + flip_core][k]

        @pl.when(row != y)
        def _():
            for t in range(2):
                right[k, :, t * width : (t + 1) * width] = cols_in[t][k]

        for at in range(0, deep, 2 * half):
            re = right[k, at : at + half, 0:columns]
            im = right[k, at + half : at + 2 * half, 0:columns]
            right[k, at : at + half, columns : 2 * columns] = -im
            right[k, at + half : at + 2 * half, columns : 2 * columns] = re
        for begin in range(0, 4, TOGETHER):
            sources = range(begin, begin + TOGETHER)
            product = lax.dot_general(
                jnp.concatenate([rows_in[source][k] for source in sources], axis=1),
                right[k],
                (((0,), (0,)), ((), ())),
                preferred_element_type=jnp.float32,
            )
            for source in sources:
                from_row = (source - begin) * width
                block = lax.rem(y + source // 2, 2) * 2 + lax.rem(core + source % 2, 2)
                to = pl.ds(pl.multiple_of(block * width, width), width)
                for q in range(2):
                    staged[q][k, source * width : (source + 1) * width, :] = product[
                        from_row : from_row + width, q * columns : (q + 1) * columns
                    ].astype(jnp.bfloat16)
                    copy = pltpu.make_async_copy(
                        staged[q].at[k, pl.ds(source * width, width), :],
                        outs[q].at[k, to, :],
                        sems.at[k, source, q],
                    )
                    copy.start()
                    copies.append(copy)
    for copy in copies:
        copy.wait()


def products(row_blocks, col_blocks, half):
    _, deep, width = row_blocks[0][0].shape
    flat = [a for part in row_blocks for a in part] + [a for part in col_blocks for a in part]
    shape = (CH_DEV, 4 * width, 2 * width)
    out = jax.ShapeDtypeStruct(shape, jnp.bfloat16)
    return pl.pallas_call(
        functools.partial(products_body, half=half),
        in_specs=[pl.BlockSpec(memory_space=pltpu.VMEM)] * len(flat),
        out_specs=[pl.BlockSpec(memory_space=pltpu.HBM)] * 2,
        out_shape=[out, out],
        scratch_shapes=[
            pltpu.VMEM((CH_DEV, deep, 4 * width), jnp.bfloat16),
            pltpu.VMEM(shape, jnp.bfloat16),
            pltpu.VMEM(shape, jnp.bfloat16),
            pltpu.SemaphoreType.DMA((CH_DEV, 4, 2)),
        ],
        compiler_params=pltpu.CompilerParams(vmem_limit_bytes=28 * 2**20),
        cost_estimate=pl.CostEstimate(
            flops=2 * CH_DEV * deep * 16 * width * width,
            bytes_accessed=2 * 2 * CH_DEV * 8 * width * width,
            transcendentals=0,
        ),
        name="products",
    )(*flat)


TOGETHER = 1


def exchange(sent, groups):
    moves = [[(i, target_of(i, s, groups)) for i in range(groups)] for s in range(groups)]
    return [sent[0]] + [lax.ppermute(sent[s], "freq", moves[s]) for s in range(1, groups)]


def gather(mine):
    other_core = [(0, 1), (1, 0), (2, 3), (3, 2)]
    other_y = [(0, 2), (2, 0), (1, 3), (3, 1)]
    place = lambda x, y, c: x * 4 + y * 2 + c
    far_y = lax.ppermute(mine, "col", other_y)
    columns = [
        lax.ppermute(
            mine,
            ("row", "col"),
            [(place(x, y, c), place(1 - x, x, y)) for x in range(2) for y in range(2)],
        )
        for c in range(2)
    ]
    near = lax.ppermute(mine, "col", other_core)
    far = lax.ppermute(far_y, "col", other_core)
    return [mine, near, far_y, far], columns


def fast(samples, input_gains, filter_taps):
    groups = lax.axis_size("freq")
    parts = PARTS
    half = SPEC // 2 // parts
    row_blocks, col_blocks = [], []
    for part in range(parts):
        sent = channelize(
            samples, input_gains, filter_taps, part * 2 * half, half, CUTS, groups
        )
        turned = exchange(sent, groups)
        turned[1] = hold(turned[1])
        mine = regroup(turned, half)
        rows, columns = gather(mine)
        row_blocks.append(rows)
        col_blocks.append(columns)
    return tuple(products(row_blocks, col_blocks, half))


PARTS = 1
CUTS = (0, 3, 7, 11, 15, 19, 23, 27, 31, 35)


def dft_table(channels):
    position = jnp.arange(NFFT, dtype=jnp.int32)
    channel = jnp.arange(channels, dtype=jnp.int32)
    phases = (position[:, None] * channel[None, :] % NFFT).astype(jnp.float32) * (
        2.0 * math.pi / NFFT
    )
    scaling = 0.5 / math.sqrt(NFFT)
    cosine = jnp.cos(phases) * scaling
    sine = jnp.sin(phases) * scaling
    real_rows = jnp.stack([cosine, -sine], axis=1)
    imag_rows = jnp.stack([sine, cosine], axis=1)
    return jnp.stack([real_rows, imag_rows], axis=0).astype(jnp.bfloat16)


def plain(samples, input_gains, filter_taps):
    channels = CH_DEV * lax.axis_size("freq")
    inputs_here = samples.shape[1]
    voltage = samples.astype(jnp.float32) * 0.25 * input_gains[None, :, None]
    frames = voltage.reshape(2, inputs_here, SPEC + TAPS - 1, NFFT)
    filtered = frames[:, :, 0:SPEC, :] * filter_taps[0]
    for tap_index in range(1, TAPS):
        filtered = filtered + frames[:, :, tap_index : tap_index + SPEC, :] * filter_taps[tap_index]
    filtered = filtered.astype(jnp.bfloat16)
    spectra = jnp.einsum(
        "pimn,pnqk->kiqm", filtered, dft_table(channels), preferred_element_type=jnp.float32
    )
    spectra = spectra.reshape(channels, inputs_here, 2 * SPEC).astype(jnp.bfloat16)
    grouped = lax.all_to_all(spectra, "freq", split_axis=0, concat_axis=1, tiled=True)
    row_count = lax.axis_size("row")
    column_count = lax.axis_size("col")
    everything = lax.all_gather(grouped, ("row", "col"), axis=1, tiled=True)
    row_size = everything.shape[1] // row_count
    column_size = everything.shape[1] // column_count
    row_data = lax.dynamic_slice_in_dim(everything, lax.axis_index("row") * row_size, row_size, 1)
    column_data = lax.dynamic_slice_in_dim(
        everything, lax.axis_index("col") * column_size, column_size, 1
    )
    rotated = jnp.concatenate([-column_data[:, :, SPEC:], column_data[:, :, :SPEC]], axis=2)
    stacked = jnp.concatenate([column_data, rotated], axis=1)
    product = jnp.einsum("kim,kjm->kij", row_data, stacked, preferred_element_type=jnp.float32) * (
        1.0 / SPEC
    )
    width = column_data.shape[1]
    vis_real = product[:, :, :width].astype(jnp.bfloat16)
    vis_imag = product[:, :, width:].astype(jnp.bfloat16)
    return (vis_real, vis_imag)


def solution(mesh):
    placed = (P(None, ("row", "col", "freq"), None), P(("row", "col", "freq")), P())
    fits = dict(mesh.shape) == {"freq": 4, "row": 2, "col": 4}
    return jax.shard_map(
        fast if fits else plain,
        mesh=mesh,
        in_specs=placed,
        out_specs=(P("freq", "row", "col"), P("freq", "row", "col")),
        check_vma=False,
    )
```

```python
import functools
import math

import jax
import jax.numpy as jnp
import numpy as np
from jax import lax
from jax.experimental import pallas as pl
from jax.experimental.pallas import tpu as pltpu
from jax.sharding import PartitionSpec as P

NFFT = 1024
TAPS = 4
SPEC = 64
CH_DEV = 4
LANES = 128
AHEAD = 2
PAD = 16
VMEM_BYTES = 60 * 2**20


SHIFTS = (0, 2, 1, 3)


def partner(me, s, groups, sign=1):
    return lax.rem(me + sign * SHIFTS[s] + groups, groups)


def target_of(i, s, groups):
    return (i + SHIFTS[s]) % groups


def dft_rows(channels):
    phases = (np.arange(channels)[:, None] * np.arange(NFFT)[None, :] % NFFT) * (
        2.0 * math.pi / NFFT
    )
    scaling = 0.5 / math.sqrt(NFFT)
    cosine = np.cos(phases) * scaling
    sine = np.sin(phases) * scaling
    real_rows = np.concatenate([cosine, sine], axis=1)
    imag_rows = np.concatenate([-sine, cosine], axis=1)
    rows = np.stack([real_rows, imag_rows], axis=1).reshape(2 * channels, 2 * NFFT)
    return jnp.asarray(rows.astype(np.float32)).astype(jnp.bfloat16)


def channelize_body(
    gain_hbm, taps_hbm, table_hbm, samples_ref, *rest, first, half, blocks, groups
):
    outs, scratch = rest[:groups], rest[groups:]
    gain_ref, taps_ref, table_ref, weights, raw, lhs, sums, held, staged = scratch[:9]
    sems, small_sems, out_sems = scratch[9:]
    inputs = samples_ref.shape[1]
    rows = table_ref.shape[0]
    small = [
        pltpu.make_async_copy(source, target, small_sems.at[index])
        for index, (source, target) in enumerate(
            [(taps_hbm, taps_ref), (table_hbm, table_ref), (gain_hbm, gain_ref)]
        )
    ]
    for copy in small:
        copy.start()
    copies = []
    for index, (start, stop) in enumerate(blocks):
        copies.append([])
        for side, begin, end in ((0, start, min(stop, half)), (1, half + start, half + stop)):
            if begin < end:
                span = pl.ds(begin * NFFT, (end - begin) * NFFT)
                source = pl.ds((first + begin) * NFFT, (end - begin) * NFFT)
                copy = pltpu.make_async_copy(
                    samples_ref.at[:, :, source], raw.at[:, :, span], sems.at[index, side]
                )
                copies[-1].append(copy)
    for index in range(min(AHEAD, len(blocks))):
        for copy in copies[index]:
            copy.start()
    for copy in small:
        copy.wait()
    for index in range(AHEAD, len(blocks)):
        for copy in copies[index]:
            copy.start()
    for p in range(2):
        for b in range(NFFT // LANES):
            table = table_ref[:, p * NFFT + b * LANES : p * NFFT + (b + 1) * LANES].astype(
                jnp.float32
            )
            for t in range(TAPS):
                exact = table * taps_ref[t : t + 1, b * LANES : (b + 1) * LANES]
                high = exact.astype(jnp.bfloat16)
                low = (exact - high.astype(jnp.float32)).astype(jnp.bfloat16)
                at = pl.ds(p * NFFT + b * LANES, LANES)
                weights[t * rows : (t + 1) * rows, at] = high
                weights[(TAPS + t) * rows : (TAPS + t + 1) * rows, at] = low
    gain = gain_ref[...]
    gain = jnp.concatenate([gain, gain], axis=1) * (0.25 / math.sqrt(SPEC))
    for index, (start, stop) in enumerate(blocks):
        for copy in copies[index]:
            copy.wait()
        buffer = lhs[index % 2]
        for slot in range(start, stop):
            for side in range(2):
                frame = side * half + slot
                to = (slot - start) * 2 * inputs + side * inputs
                for p in range(2):
                    buffer[to : to + inputs, p * NFFT : (p + 1) * NFFT] = (
                        raw[p, :, frame * NFFT : (frame + 1) * NFFT]
                        .astype(jnp.float32)
                        .astype(jnp.bfloat16)
                    )
        size = (stop - start) * 2 * inputs
        both = lax.dot_general(
            weights[...],
            buffer[0:size, :],
            (((1,), (1,)), ((), ())),
            preferred_element_type=jnp.float32,
        )
        sums[:, start * LANES : stop * LANES] = both[: TAPS * rows] + both[TAPS * rows :]
        for slot in range(max(start - TAPS + 1, 0), stop - TAPS + 1):
            total = sums[0:rows, slot * LANES : (slot + 1) * LANES]
            for t in range(1, TAPS):
                total = total + sums[
                    t * rows : (t + 1) * rows, (slot + t) * LANES : (slot + t + 1) * LANES
                ]
            held[pl.ds(slot, rows, stride=half), :] = total * gain
    me = lax.axis_index("freq")
    depth = 2 * half
    sent = []
    for s in range(groups):
        to = partner(me, s, groups) * (CH_DEV * depth)
        size = CH_DEV * depth
        staged[s, 0:size] = held[pl.ds(pl.multiple_of(to, 8), size), :].astype(jnp.bfloat16)
        if s:
            staged[s, size : size + PAD] = jnp.zeros((PAD, LANES), jnp.bfloat16)
            size += PAD
        sent.append(
            pltpu.make_async_copy(staged.at[s, pl.ds(0, size), :], outs[s], out_sems.at[s])
        )
        sent[-1].start()
    for copy in sent:
        copy.wait()


def channelize(samples, gains, taps, first, half, cuts, groups):
    inputs = samples.shape[1]
    channels = CH_DEV * groups
    rows = 2 * channels
    slots = half + TAPS - 1
    blocks = list(zip(cuts[:-1], cuts[1:]))
    widest = max(stop - start for start, stop in blocks)
    frames = 2 * half + TAPS - 1
    return pl.pallas_call(
        functools.partial(
            channelize_body, first=first, half=half, blocks=blocks, groups=groups
        ),
        in_specs=[pl.BlockSpec(memory_space=pltpu.HBM)] * 4,
        out_specs=[pl.BlockSpec(memory_space=pltpu.HBM)] * groups,
        out_shape=[
            jax.ShapeDtypeStruct((CH_DEV * 2 * half + (PAD if s else 0), LANES), jnp.bfloat16)
            for s in range(groups)
        ],
        scratch_shapes=[
            pltpu.VMEM((1, inputs), jnp.float32),
            pltpu.VMEM((TAPS, NFFT), jnp.float32),
            pltpu.VMEM((rows, 2 * NFFT), jnp.bfloat16),
            pltpu.VMEM((2 * TAPS * rows, 2 * NFFT), jnp.bfloat16),
            pltpu.VMEM((2, inputs, frames * NFFT), jnp.int32),
            [pltpu.VMEM((widest * 2 * inputs, 2 * NFFT), jnp.bfloat16)] * 2,
            pltpu.VMEM((TAPS * rows, slots * LANES), jnp.float32),
            pltpu.VMEM((rows * half, LANES), jnp.float32),
            pltpu.VMEM((groups, CH_DEV * 2 * half + PAD, LANES), jnp.bfloat16),
            pltpu.SemaphoreType.DMA((len(blocks), 2)),
            pltpu.SemaphoreType.DMA((3,)),
            pltpu.SemaphoreType.DMA((groups,)),
        ],
        compiler_params=pltpu.CompilerParams(vmem_limit_bytes=VMEM_BYTES),
        cost_estimate=pl.CostEstimate(
            flops=2 * 2 * NFFT * 256 * frames * inputs,
            bytes_accessed=8 * inputs * frames * NFFT,
            transcendentals=0,
        ),
        name="channelize",
    )(gains.reshape(1, inputs), taps, dft_rows(channels), samples)


def hold_body(source, out):
    out[...] = source[...]


def hold(array):
    return pl.pallas_call(
        hold_body,
        out_shape=jax.ShapeDtypeStruct(array.shape, array.dtype),
        in_specs=[pl.BlockSpec(memory_space=pltpu.VMEM)],
        out_specs=pl.BlockSpec(memory_space=pltpu.VMEM),
        compiler_params=pltpu.CompilerParams(vmem_limit_bytes=2 * 2**20),
        cost_estimate=pl.CostEstimate(flops=4 * 10**10, bytes_accessed=0, transcendentals=0),
        name="hold",
    )(array)


def regroup_body(*refs, half, groups):
    sources, out, ordered = refs[:-2], refs[-2], refs[-1]
    me = lax.axis_index("freq")
    depth = 2 * half
    size = CH_DEV * depth
    for s in range(groups):
        if len(sources) == groups:
            piece = sources[s][0:size]
        else:
            piece = sources[1][(s - 1) * size : s * size] if s else sources[0][...]
        ordered[partner(me, s, groups, -1)] = piece
    lane = lax.broadcasted_iota(jnp.int32, (depth, LANES), 1)
    for pair in range(groups // 2):
        for k in range(CH_DEV):
            rows = slice(k * depth, (k + 1) * depth)
            left = ordered[2 * pair, rows].astype(jnp.float32)
            right = ordered[2 * pair + 1, rows].astype(jnp.float32)
            early = jnp.where(lane < LANES // 2, left, pltpu.roll(right, LANES // 2, 1))
            late = jnp.where(lane < LANES // 2, pltpu.roll(left, LANES // 2, 1), right)
            at = pl.ds(pair * LANES, LANES)
            out[k, 0:depth, at] = early.astype(jnp.bfloat16)
            out[k, depth : 2 * depth, at] = late.astype(jnp.bfloat16)


def regroup(sources, half, groups):
    shape = (CH_DEV, 4 * half, groups * LANES // 2)
    return pl.pallas_call(
        functools.partial(regroup_body, half=half, groups=groups),
        out_shape=jax.ShapeDtypeStruct(shape, jnp.bfloat16),
        scratch_shapes=[pltpu.VMEM((groups, CH_DEV * 2 * half, LANES), jnp.bfloat16)],
        compiler_params=pltpu.CompilerParams(vmem_limit_bytes=4 * 2**20),
        name="regroup",
    )(*sources)


def stack_body(*refs, count):
    size = refs[-1].shape[0] // count
    for index in range(count):
        refs[-1][index * size : (index + 1) * size] = refs[index][0:size]


def stack(pieces, after):
    rows, lanes = pieces[0].shape
    return pl.pallas_call(
        functools.partial(stack_body, count=len(pieces)),
        out_shape=jax.ShapeDtypeStruct((len(pieces) * (rows - PAD), lanes), jnp.bfloat16),
        in_specs=[pl.BlockSpec(memory_space=pltpu.VMEM)] * len(pieces)
        + [pl.BlockSpec(memory_space=pl.ANY)] * len(after),
        out_specs=pl.BlockSpec(memory_space=pltpu.VMEM),
        compiler_params=pltpu.CompilerParams(vmem_limit_bytes=2 * 2**20),
        name="stack",
    )(*pieces, *after)


def products_body(*refs, half):
    rows_in, cols_in = refs[0:4], refs[4:6]
    outs, right, staged, sems = refs[6:8], refs[8], refs[9:11], refs[11]
    row, col = lax.axis_index("row"), lax.axis_index("col")
    y, core = col // 2, lax.rem(col, 2)
    deep, width = rows_in[0].shape[1:]
    columns = 2 * width
    copies = []
    for k in range(CH_DEV):
        for flip_y in range(2):

            @pl.when((row == y) & ((core != y) if flip_y else (core == y)))
            def _():
                for flip_core in range(2):
                    at = pl.multiple_of(lax.rem(core + flip_core, 2) * width, width)
                    right[k, :, pl.ds(at, width)] = rows_in[2 * flip_y + flip_core][k]

        @pl.when(row != y)
        def _():
            for t in range(2):
                right[k, :, t * width : (t + 1) * width] = cols_in[t][k]

        for at in range(0, deep, 2 * half):
            re = right[k, at : at + half, 0:columns]
            im = right[k, at + half : at + 2 * half, 0:columns]
            right[k, at : at + half, columns : 2 * columns] = -im
            right[k, at + half : at + 2 * half, columns : 2 * columns] = re
        for begin in range(0, 4, TOGETHER):
            sources = range(begin, begin + TOGETHER)
            product = lax.dot_general(
                jnp.concatenate([rows_in[source][k] for source in sources], axis=1),
                right[k],
                (((0,), (0,)), ((), ())),
                preferred_element_type=jnp.float32,
            )
            for source in sources:
                from_row = (source - begin) * width
                block = lax.rem(y + source // 2, 2) * 2 + lax.rem(core + source % 2, 2)
                to = pl.ds(pl.multiple_of(block * width, width), width)
                for q in range(2):
                    staged[q][k, source * width : (source + 1) * width, :] = product[
                        from_row : from_row + width, q * columns : (q + 1) * columns
                    ].astype(jnp.bfloat16)
                    copy = pltpu.make_async_copy(
                        staged[q].at[k, pl.ds(source * width, width), :],
                        outs[q].at[k, to, :],
                        sems.at[k, source, q],
                    )
                    copy.start()
                    copies.append(copy)
    for copy in copies:
        copy.wait()


def products(row_blocks, col_blocks, half):
    _, deep, width = row_blocks[0][0].shape
    flat = [a for part in row_blocks for a in part] + [a for part in col_blocks for a in part]
    shape = (CH_DEV, 4 * width, 2 * width)
    out = jax.ShapeDtypeStruct(shape, jnp.bfloat16)
    return pl.pallas_call(
        functools.partial(products_body, half=half),
        in_specs=[pl.BlockSpec(memory_space=pltpu.VMEM)] * len(flat),
        out_specs=[pl.BlockSpec(memory_space=pltpu.HBM)] * 2,
        out_shape=[out, out],
        scratch_shapes=[
            pltpu.VMEM((CH_DEV, deep, 4 * width), jnp.bfloat16),
            pltpu.VMEM(shape, jnp.bfloat16),
            pltpu.VMEM(shape, jnp.bfloat16),
            pltpu.SemaphoreType.DMA((CH_DEV, 4, 2)),
        ],
        compiler_params=pltpu.CompilerParams(vmem_limit_bytes=28 * 2**20),
        cost_estimate=pl.CostEstimate(
            flops=2 * CH_DEV * deep * 16 * width * width,
            bytes_accessed=2 * 2 * CH_DEV * 8 * width * width,
            transcendentals=0,
        ),
        name="products",
    )(*flat)


TOGETHER = 1


def exchange(sent, groups):
    moves = [[(i, target_of(i, s, groups)) for i in range(groups)] for s in range(groups)]
    return [sent[0]] + [lax.ppermute(sent[s], "freq", moves[s]) for s in range(1, groups)]


def to_columns(mine, core):
    place = lambda x, y, c: x * 4 + y * 2 + c
    pairs = [(place(x, y, core), place(1 - x, x, y)) for x in range(2) for y in range(2)]
    return lax.ppermute(mine, ("row", "col"), pairs)


def fast(samples, input_gains, filter_taps):
    groups = lax.axis_size("freq")
    half = SPEC // 2
    other_core = [(0, 1), (1, 0), (2, 3), (3, 2)]
    other_y = [(0, 2), (2, 0), (1, 3), (3, 1)]
    sent = channelize(samples, input_gains, filter_taps, 0, half, CUTS, groups)
    turned = exchange(sent, groups)
    turned[1] = hold(turned[1])
    across_own = lax.ppermute(turned[0], "col", other_y)
    mine = regroup(turned, half, groups)
    across_rest = lax.ppermute(stack(turned[1:], [across_own, mine]), "col", other_y)
    columns = [to_columns(mine, core) for core in range(2)]
    near = lax.ppermute(mine, "col", other_core)
    across = regroup([across_own, across_rest], half, groups)
    far = lax.ppermute(across, "col", other_core)
    return tuple(products([(mine, near, across, far)], [columns], half))


CUTS = (0, 3, 8, 13, 18, 23, 27, 31, 35)


def dft_table(channels):
    position = jnp.arange(NFFT, dtype=jnp.int32)
    channel = jnp.arange(channels, dtype=jnp.int32)
    phases = (position[:, None] * channel[None, :] % NFFT).astype(jnp.float32) * (
        2.0 * math.pi / NFFT
    )
    scaling = 0.5 / math.sqrt(NFFT)
    cosine = jnp.cos(phases) * scaling
    sine = jnp.sin(phases) * scaling
    real_rows = jnp.stack([cosine, -sine], axis=1)
    imag_rows = jnp.stack([sine, cosine], axis=1)
    return jnp.stack([real_rows, imag_rows], axis=0).astype(jnp.bfloat16)


def plain(samples, input_gains, filter_taps):
    channels = CH_DEV * lax.axis_size("freq")
    inputs_here = samples.shape[1]
    voltage = samples.astype(jnp.float32) * 0.25 * input_gains[None, :, None]
    frames = voltage.reshape(2, inputs_here, SPEC + TAPS - 1, NFFT)
    filtered = frames[:, :, 0:SPEC, :] * filter_taps[0]
    for tap_index in range(1, TAPS):
        filtered = filtered + frames[:, :, tap_index : tap_index + SPEC, :] * filter_taps[tap_index]
    filtered = filtered.astype(jnp.bfloat16)
    spectra = jnp.einsum(
        "pimn,pnqk->kiqm", filtered, dft_table(channels), preferred_element_type=jnp.float32
    )
    spectra = spectra.reshape(channels, inputs_here, 2 * SPEC).astype(jnp.bfloat16)
    grouped = lax.all_to_all(spectra, "freq", split_axis=0, concat_axis=1, tiled=True)
    row_count = lax.axis_size("row")
    column_count = lax.axis_size("col")
    everything = lax.all_gather(grouped, ("row", "col"), axis=1, tiled=True)
    row_size = everything.shape[1] // row_count
    column_size = everything.shape[1] // column_count
    row_data = lax.dynamic_slice_in_dim(everything, lax.axis_index("row") * row_size, row_size, 1)
    column_data = lax.dynamic_slice_in_dim(
        everything, lax.axis_index("col") * column_size, column_size, 1
    )
    rotated = jnp.concatenate([-column_data[:, :, SPEC:], column_data[:, :, :SPEC]], axis=2)
    stacked = jnp.concatenate([column_data, rotated], axis=1)
    product = jnp.einsum("kim,kjm->kij", row_data, stacked, preferred_element_type=jnp.float32) * (
        1.0 / SPEC
    )
    width = column_data.shape[1]
    vis_real = product[:, :, :width].astype(jnp.bfloat16)
    vis_imag = product[:, :, width:].astype(jnp.bfloat16)
    return (vis_real, vis_imag)


def solution(mesh):
    placed = (P(None, ("row", "col", "freq"), None), P(("row", "col", "freq")), P())
    fits = dict(mesh.shape) == {"freq": 4, "row": 2, "col": 4}
    return jax.shard_map(
        fast if fits else plain,
        mesh=mesh,
        in_specs=placed,
        out_specs=(P("freq", "row", "col"), P("freq", "row", "col")),
        check_vma=False,
    )
```

```python
import functools
import math

import jax
import jax.numpy as jnp
import numpy as np
from jax import lax
from jax.experimental import pallas as pl
from jax.experimental.pallas import tpu as pltpu
from jax.sharding import PartitionSpec as P

NFFT = 1024
TAPS = 4
SPEC = 64
CH_DEV = 4
LANES = 128
AHEAD = 2
PAD = 16
VMEM_BYTES = 60 * 2**20


SHIFTS = (0, 1, 2, 3)


def partner(me, s, groups, sign=1):
    return lax.rem(me + sign * SHIFTS[s] + groups, groups)


def target_of(i, s, groups):
    return (i + SHIFTS[s]) % groups


def dft_rows(channels):
    phases = (np.arange(channels)[:, None] * np.arange(NFFT)[None, :] % NFFT) * (
        2.0 * math.pi / NFFT
    )
    scaling = 0.5 / math.sqrt(NFFT)
    cosine = np.cos(phases) * scaling
    sine = np.sin(phases) * scaling
    real_rows = np.concatenate([cosine, sine], axis=1)
    imag_rows = np.concatenate([-sine, cosine], axis=1)
    rows = np.stack([real_rows, imag_rows], axis=1).reshape(2 * channels, 2 * NFFT)
    return jnp.asarray(rows.astype(np.float32)).astype(jnp.bfloat16)


def channelize_body(
    gain_hbm, taps_hbm, table_hbm, samples_ref, *rest, first, half, blocks, groups
):
    outs, scratch = rest[:groups], rest[groups:]
    gain_ref, taps_ref, table_ref, weights, raw, lhs, sums, held, staged = scratch[:9]
    sems, small_sems, out_sems = scratch[9:]
    inputs = samples_ref.shape[1]
    rows = table_ref.shape[0]
    small = [
        pltpu.make_async_copy(source, target, small_sems.at[index])
        for index, (source, target) in enumerate(
            [(taps_hbm, taps_ref), (table_hbm, table_ref), (gain_hbm, gain_ref)]
        )
    ]
    for copy in small:
        copy.start()
    copies = []
    for index, (start, stop) in enumerate(blocks):
        copies.append([])
        for side, begin, end in ((0, start, min(stop, half)), (1, half + start, half + stop)):
            if begin < end:
                span = pl.ds(begin * NFFT, (end - begin) * NFFT)
                source = pl.ds((first + begin) * NFFT, (end - begin) * NFFT)
                copy = pltpu.make_async_copy(
                    samples_ref.at[:, :, source], raw.at[:, :, span], sems.at[index, side]
                )
                copies[-1].append(copy)
    for index in range(min(AHEAD, len(blocks))):
        for copy in copies[index]:
            copy.start()
    for copy in small:
        copy.wait()
    for index in range(AHEAD, len(blocks)):
        for copy in copies[index]:
            copy.start()
    for p in range(2):
        for b in range(NFFT // LANES):
            table = table_ref[:, p * NFFT + b * LANES : p * NFFT + (b + 1) * LANES].astype(
                jnp.float32
            )
            for t in range(TAPS):
                exact = table * taps_ref[t : t + 1, b * LANES : (b + 1) * LANES]
                high = exact.astype(jnp.bfloat16)
                low = (exact - high.astype(jnp.float32)).astype(jnp.bfloat16)
                at = pl.ds(p * NFFT + b * LANES, LANES)
                weights[t * rows : (t + 1) * rows, at] = high
                weights[(TAPS + t) * rows : (TAPS + t + 1) * rows, at] = low
    gain = gain_ref[...]
    gain = jnp.concatenate([gain, gain], axis=1) * (0.25 / math.sqrt(SPEC))
    for index, (start, stop) in enumerate(blocks):
        for copy in copies[index]:
            copy.wait()
        buffer = lhs[index % 2]
        for slot in range(start, stop):
            for side in range(2):
                frame = side * half + slot
                to = (slot - start) * 2 * inputs + side * inputs
                for p in range(2):
                    buffer[to : to + inputs, p * NFFT : (p + 1) * NFFT] = (
                        raw[p, :, frame * NFFT : (frame + 1) * NFFT]
                        .astype(jnp.float32)
                        .astype(jnp.bfloat16)
                    )
        size = (stop - start) * 2 * inputs
        both = lax.dot_general(
            weights[...],
            buffer[0:size, :],
            (((1,), (1,)), ((), ())),
            preferred_element_type=jnp.float32,
        )
        sums[:, start * LANES : stop * LANES] = both[: TAPS * rows] + both[TAPS * rows :]
        for slot in range(max(start - TAPS + 1, 0), stop - TAPS + 1):
            total = sums[0:rows, slot * LANES : (slot + 1) * LANES]
            for t in range(1, TAPS):
                total = total + sums[
                    t * rows : (t + 1) * rows, (slot + t) * LANES : (slot + t + 1) * LANES
                ]
            held[pl.ds(slot, rows, stride=half), :] = total * gain
    me = lax.axis_index("freq")
    depth = 2 * half
    sent = []
    for s in range(groups):
        to = partner(me, s, groups) * (CH_DEV * depth)
        size = CH_DEV * depth
        staged[s, 0:size] = held[pl.ds(pl.multiple_of(to, 8), size), :].astype(jnp.bfloat16)
        if s:
            staged[s, size : size + PAD] = jnp.zeros((PAD, LANES), jnp.bfloat16)
            size += PAD
        sent.append(
            pltpu.make_async_copy(staged.at[s, pl.ds(0, size), :], outs[s], out_sems.at[s])
        )
        sent[-1].start()
    for copy in sent:
        copy.wait()


def channelize(samples, gains, taps, first, half, cuts, groups):
    inputs = samples.shape[1]
    channels = CH_DEV * groups
    rows = 2 * channels
    slots = half + TAPS - 1
    blocks = list(zip(cuts[:-1], cuts[1:]))
    widest = max(stop - start for start, stop in blocks)
    frames = 2 * half + TAPS - 1
    return pl.pallas_call(
        functools.partial(
            channelize_body, first=first, half=half, blocks=blocks, groups=groups
        ),
        in_specs=[pl.BlockSpec(memory_space=pltpu.HBM)] * 4,
        out_specs=[pl.BlockSpec(memory_space=pltpu.HBM)] * groups,
        out_shape=[
            jax.ShapeDtypeStruct((CH_DEV * 2 * half + (PAD if s else 0), LANES), jnp.bfloat16)
            for s in range(groups)
        ],
        scratch_shapes=[
            pltpu.VMEM((1, inputs), jnp.float32),
            pltpu.VMEM((TAPS, NFFT), jnp.float32),
            pltpu.VMEM((rows, 2 * NFFT), jnp.bfloat16),
            pltpu.VMEM((2 * TAPS * rows, 2 * NFFT), jnp.bfloat16),
            pltpu.VMEM((2, inputs, frames * NFFT), jnp.int32),
            [pltpu.VMEM((widest * 2 * inputs, 2 * NFFT), jnp.bfloat16)] * 2,
            pltpu.VMEM((TAPS * rows, slots * LANES), jnp.float32),
            pltpu.VMEM((rows * half, LANES), jnp.float32),
            pltpu.VMEM((groups, CH_DEV * 2 * half + PAD, LANES), jnp.bfloat16),
            pltpu.SemaphoreType.DMA((len(blocks), 2)),
            pltpu.SemaphoreType.DMA((3,)),
            pltpu.SemaphoreType.DMA((groups,)),
        ],
        compiler_params=pltpu.CompilerParams(vmem_limit_bytes=VMEM_BYTES),
        cost_estimate=pl.CostEstimate(
            flops=2 * 2 * NFFT * 256 * frames * inputs,
            bytes_accessed=8 * inputs * frames * NFFT,
            transcendentals=0,
        ),
        name="channelize",
    )(gains.reshape(1, inputs), taps, dft_rows(channels), samples)


def hold_body(source, out):
    out[...] = source[...]


def hold(array):
    return pl.pallas_call(
        hold_body,
        out_shape=jax.ShapeDtypeStruct(array.shape, array.dtype),
        in_specs=[pl.BlockSpec(memory_space=pltpu.VMEM)],
        out_specs=pl.BlockSpec(memory_space=pltpu.VMEM),
        compiler_params=pltpu.CompilerParams(vmem_limit_bytes=2 * 2**20),
        cost_estimate=pl.CostEstimate(flops=4 * 10**10, bytes_accessed=0, transcendentals=0),
        name="hold",
    )(array)


def regroup_body(*refs, half, groups):
    sources, out, ordered = refs[:-2], refs[-2], refs[-1]
    me = lax.axis_index("freq")
    depth = 2 * half
    size = CH_DEV * depth
    for s in range(groups):
        if len(sources) == groups:
            piece = sources[s][0:size]
        else:
            piece = sources[1][(s - 1) * size : s * size] if s else sources[0][...]
        ordered[partner(me, s, groups, -1)] = piece
    lane = lax.broadcasted_iota(jnp.int32, (depth, LANES), 1)
    for pair in range(groups // 2):
        for k in range(CH_DEV):
            rows = slice(k * depth, (k + 1) * depth)
            left = ordered[2 * pair, rows].astype(jnp.float32)
            right = ordered[2 * pair + 1, rows].astype(jnp.float32)
            early = jnp.where(lane < LANES // 2, left, pltpu.roll(right, LANES // 2, 1))
            late = jnp.where(lane < LANES // 2, pltpu.roll(left, LANES // 2, 1), right)
            at = pl.ds(pair * LANES, LANES)
            out[k, 0:depth, at] = early.astype(jnp.bfloat16)
            out[k, depth : 2 * depth, at] = late.astype(jnp.bfloat16)


def regroup(sources, half, groups):
    shape = (CH_DEV, 4 * half, groups * LANES // 2)
    return pl.pallas_call(
        functools.partial(regroup_body, half=half, groups=groups),
        out_shape=jax.ShapeDtypeStruct(shape, jnp.bfloat16),
        scratch_shapes=[pltpu.VMEM((groups, CH_DEV * 2 * half, LANES), jnp.bfloat16)],
        compiler_params=pltpu.CompilerParams(vmem_limit_bytes=4 * 2**20),
        name="regroup",
    )(*sources)


def stack_body(*refs, count):
    size = refs[-1].shape[0] // count
    for index in range(count):
        refs[-1][index * size : (index + 1) * size] = refs[index][0:size]


def stack(pieces, after):
    rows, lanes = pieces[0].shape
    return pl.pallas_call(
        functools.partial(stack_body, count=len(pieces)),
        out_shape=jax.ShapeDtypeStruct((len(pieces) * (rows - PAD), lanes), jnp.bfloat16),
        in_specs=[pl.BlockSpec(memory_space=pltpu.VMEM)] * len(pieces)
        + [pl.BlockSpec(memory_space=pl.ANY)] * len(after),
        out_specs=pl.BlockSpec(memory_space=pltpu.VMEM),
        compiler_params=pltpu.CompilerParams(vmem_limit_bytes=2 * 2**20),
        name="stack",
    )(*pieces, *after)


def products_body(*refs, half):
    rows_in, cols_in = refs[0:4], refs[4:6]
    outs, right, staged, sems = refs[6:8], refs[8], refs[9:11], refs[11]
    row, col = lax.axis_index("row"), lax.axis_index("col")
    y, core = col // 2, lax.rem(col, 2)
    deep, width = rows_in[0].shape[1:]
    columns = 2 * width
    copies = []
    for k in range(CH_DEV):
        for flip_y in range(2):

            @pl.when((row == y) & ((core != y) if flip_y else (core == y)))
            def _():
                for flip_core in range(2):
                    at = pl.multiple_of(lax.rem(core + flip_core, 2) * width, width)
                    right[k, :, pl.ds(at, width)] = rows_in[2 * flip_y + flip_core][k]

        @pl.when(row != y)
        def _():
            for t in range(2):
                right[k, :, t * width : (t + 1) * width] = cols_in[t][k]

        for at in range(0, deep, 2 * half):
            re = right[k, at : at + half, 0:columns]
            im = right[k, at + half : at + 2 * half, 0:columns]
            right[k, at : at + half, columns : 2 * columns] = -im
            right[k, at + half : at + 2 * half, columns : 2 * columns] = re
        for begin in range(0, 4, TOGETHER):
            sources = range(begin, begin + TOGETHER)
            product = lax.dot_general(
                jnp.concatenate([rows_in[source][k] for source in sources], axis=1),
                right[k],
                (((0,), (0,)), ((), ())),
                preferred_element_type=jnp.float32,
            )
            for source in sources:
                from_row = (source - begin) * width
                block = lax.rem(y + source // 2, 2) * 2 + lax.rem(core + source % 2, 2)
                to = pl.ds(pl.multiple_of(block * width, width), width)
                for q in range(2):
                    staged[q][k, source * width : (source + 1) * width, :] = product[
                        from_row : from_row + width, q * columns : (q + 1) * columns
                    ].astype(jnp.bfloat16)
                    copy = pltpu.make_async_copy(
                        staged[q].at[k, pl.ds(source * width, width), :],
                        outs[q].at[k, to, :],
                        sems.at[k, source, q],
                    )
                    copy.start()
                    copies.append(copy)
    for copy in copies:
        copy.wait()


def products(row_blocks, col_blocks, half):
    _, deep, width = row_blocks[0][0].shape
    flat = [a for part in row_blocks for a in part] + [a for part in col_blocks for a in part]
    shape = (CH_DEV, 4 * width, 2 * width)
    out = jax.ShapeDtypeStruct(shape, jnp.bfloat16)
    return pl.pallas_call(
        functools.partial(products_body, half=half),
        in_specs=[pl.BlockSpec(memory_space=pltpu.VMEM)] * len(flat),
        out_specs=[pl.BlockSpec(memory_space=pltpu.HBM)] * 2,
        out_shape=[out, out],
        scratch_shapes=[
            pltpu.VMEM((CH_DEV, deep, 4 * width), jnp.bfloat16),
            pltpu.VMEM(shape, jnp.bfloat16),
            pltpu.VMEM(shape, jnp.bfloat16),
            pltpu.SemaphoreType.DMA((CH_DEV, 4, 2)),
        ],
        compiler_params=pltpu.CompilerParams(vmem_limit_bytes=28 * 2**20),
        cost_estimate=pl.CostEstimate(
            flops=2 * CH_DEV * deep * 16 * width * width,
            bytes_accessed=2 * 2 * CH_DEV * 8 * width * width,
            transcendentals=0,
        ),
        name="products",
    )(*flat)


TOGETHER = 1


def exchange(sent, groups):
    moves = [[(i, target_of(i, s, groups)) for i in range(groups)] for s in range(groups)]
    return [sent[0]] + [lax.ppermute(sent[s], "freq", moves[s]) for s in range(1, groups)]


def to_columns(mine, core):
    place = lambda x, y, c: x * 4 + y * 2 + c
    pairs = [(place(x, y, core), place(1 - x, x, y)) for x in range(2) for y in range(2)]
    return lax.ppermute(mine, ("row", "col"), pairs)


def fast(samples, input_gains, filter_taps):
    groups = lax.axis_size("freq")
    half = SPEC // 2
    other_core = [(0, 1), (1, 0), (2, 3), (3, 2)]
    other_y = [(0, 2), (2, 0), (1, 3), (3, 1)]
    sent = channelize(samples, input_gains, filter_taps, 0, half, CUTS, groups)
    turned = exchange(sent, groups)
    turned[1] = hold(turned[1])
    across_own = lax.ppermute(turned[0], "col", other_y)
    mine = regroup(turned, half, groups)
    across_rest = lax.ppermute(stack(turned[1:], [across_own, mine]), "col", other_y)
    columns = [to_columns(mine, core) for core in range(2)]
    near = lax.ppermute(mine, "col", other_core)
    across = regroup([across_own, across_rest], half, groups)
    far = lax.ppermute(across, "col", other_core)
    return tuple(products([(mine, near, across, far)], [columns], half))


CUTS = (0, 3, 8, 13, 18, 23, 27, 31, 35)


def dft_table(channels):
    position = jnp.arange(NFFT, dtype=jnp.int32)
    channel = jnp.arange(channels, dtype=jnp.int32)
    phases = (position[:, None] * channel[None, :] % NFFT).astype(jnp.float32) * (
        2.0 * math.pi / NFFT
    )
    scaling = 0.5 / math.sqrt(NFFT)
    cosine = jnp.cos(phases) * scaling
    sine = jnp.sin(phases) * scaling
    real_rows = jnp.stack([cosine, -sine], axis=1)
    imag_rows = jnp.stack([sine, cosine], axis=1)
    return jnp.stack([real_rows, imag_rows], axis=0).astype(jnp.bfloat16)


def plain(samples, input_gains, filter_taps):
    channels = CH_DEV * lax.axis_size("freq")
    inputs_here = samples.shape[1]
    voltage = samples.astype(jnp.float32) * 0.25 * input_gains[None, :, None]
    frames = voltage.reshape(2, inputs_here, SPEC + TAPS - 1, NFFT)
    filtered = frames[:, :, 0:SPEC, :] * filter_taps[0]
    for tap_index in range(1, TAPS):
        filtered = filtered + frames[:, :, tap_index : tap_index + SPEC, :] * filter_taps[tap_index]
    filtered = filtered.astype(jnp.bfloat16)
    spectra = jnp.einsum(
        "pimn,pnqk->kiqm", filtered, dft_table(channels), preferred_element_type=jnp.float32
    )
    spectra = spectra.reshape(channels, inputs_here, 2 * SPEC).astype(jnp.bfloat16)
    grouped = lax.all_to_all(spectra, "freq", split_axis=0, concat_axis=1, tiled=True)
    row_count = lax.axis_size("row")
    column_count = lax.axis_size("col")
    everything = lax.all_gather(grouped, ("row", "col"), axis=1, tiled=True)
    row_size = everything.shape[1] // row_count
    column_size = everything.shape[1] // column_count
    row_data = lax.dynamic_slice_in_dim(everything, lax.axis_index("row") * row_size, row_size, 1)
    column_data = lax.dynamic_slice_in_dim(
        everything, lax.axis_index("col") * column_size, column_size, 1
    )
    rotated = jnp.concatenate([-column_data[:, :, SPEC:], column_data[:, :, :SPEC]], axis=2)
    stacked = jnp.concatenate([column_data, rotated], axis=1)
    product = jnp.einsum("kim,kjm->kij", row_data, stacked, preferred_element_type=jnp.float32) * (
        1.0 / SPEC
    )
    width = column_data.shape[1]
    vis_real = product[:, :, :width].astype(jnp.bfloat16)
    vis_imag = product[:, :, width:].astype(jnp.bfloat16)
    return (vis_real, vis_imag)


def solution(mesh):
    placed = (P(None, ("row", "col", "freq"), None), P(("row", "col", "freq")), P())
    fits = dict(mesh.shape) == {"freq": 4, "row": 2, "col": 4}
    return jax.shard_map(
        fast if fits else plain,
        mesh=mesh,
        in_specs=placed,
        out_specs=(P("freq", "row", "col"), P("freq", "row", "col")),
        check_vma=False,
    )
```
